32 devices in a mesh: group: 8 (over z, y), inner: 4 (over x, core).
Axes of the slice: x: 2, y: 2, z: 4, core: 2. Of those that a mesh axis runs over, the one named last changes fastest.
Arguments:
- tokens: bfloat16 [4096, 7168], P(('group', 'inner')), may hold values from -6 to 6
- target: int32 [4096], P(('group', 'inner')), may hold values from 0 to 8, as said below
- gate_scale: float32 [4096], P(('group', 'inner')), may hold values from 0.25 to 2.5
- gate_weight: bfloat16 [8, 7168, 2048], P('group', None, 'inner'), may hold values from -0.0625 to 0.0625
- up_weight: bfloat16 [8, 7168, 2048], P('group', None, 'inner'), may hold values from -0.0625 to 0.0625
- down_weight: bfloat16 [8, 2048, 7168], P('group', 'inner'), may hold values from -0.125 to 0.125
Outputs:
- routed_out: bfloat16 [4096, 7168], P(('group', 'inner'))
The draws below stay inside these ranges and needn't reach their ends.
Inputs may be any that keep to these rules, and one draw needn't show every extreme that they name: 8 means that the token uses no expert of this round. Among the 128 tokens of one device at most 20 target any one group, and in every device some group is targeted by exactly 20 of them.
All inputs are finite; a program needn't handle non-finite values.
Results may differ from the reference program's by a relative error of at most 0.0095.
Values may be sent and summed in bfloat16 or wider, within the bound.
No kernel may reach another device: no remote copies, remote signals or barrier semaphores. Data moves between devices by JAX's collectives and lax.ppermute only.
A program may use at most 192 MiB of HBM per device.

```python
import math
import jax
import jax.numpy as jnp
from jax import lax

D = 7168
FF = 2048
TOK_DEV = 128
EXPERTS = 8
CAP = 20
TOKENS = 4096
N_GROUP = 8
N_INNER = 4


def draw_target(key, part):
    blocks = N_GROUP * N_INNER
    key_hot, key_raw, key_mix = jax.random.split(jax.random.fold_in(key, 11), 3)
    hot_group = jax.random.randint(key_hot, (blocks, 1), 0, N_GROUP)
    raw_pick = jax.random.randint(key_raw, (blocks, TOK_DEV), 0, 2 * N_GROUP)
    position = jnp.arange(TOK_DEV, dtype=jnp.int32)[None, :]
    wanted = jnp.where(position < CAP, hot_group, raw_pick)
    wanted = jnp.where(wanted >= N_GROUP, N_GROUP, wanted)
    onehot = (wanted[:, :, None] == jnp.arange(N_GROUP, dtype=jnp.int32)[None, None, :]).astype(jnp.int32)
    before = jnp.sum((jnp.cumsum(onehot, axis=1) - onehot) * onehot, axis=2)
    wanted = jnp.where(before >= CAP, N_GROUP, wanted)
    scores = jax.random.randint(key_mix, (blocks, TOK_DEV), 0, 1 << 20) * TOK_DEV + position
    ordering = jnp.argsort(scores, axis=1, stable=True)
    return jnp.take_along_axis(wanted, ordering, axis=1).reshape(blocks * TOK_DEV).astype(jnp.int32)


def levels(rng, dims, shards, smallest, high):
    level = 1.0
    for dim, blocks in shards:
        steps = jax.random.uniform(jax.random.fold_in(jax.random.fold_in(rng, 6), dim), (blocks,), jnp.float32, smallest / len(shards), high / len(shards))
        level = level * jnp.repeat(jnp.exp(steps), dims[dim] // blocks).reshape((-1,) + (1,) * (len(dims) - 1 - dim))
    return level


def normal_values(stream_key, dims, width, limit, shards=(), kind=jnp.bfloat16):
    array = jax.random.normal(stream_key, dims, jnp.float32) * width
    if len(shards) > 0:
        array = levels(stream_key, dims, shards, -0.22, 0.18) * array
    return jnp.clip(array, min=-limit, max=limit).astype(kind)


def setup_inputs(seed: int = 0) -> dict:
    streams_of = jax.random.split(jax.random.key(seed), 7)
    return {
        "tokens": normal_values(streams_of[0], (TOKENS, D), 1.0, 6.0, ((0, 32),)),
        "target": draw_target(jax.random.fold_in(streams_of[6], 71), 0),
        "gate_scale": jnp.clip(jnp.exp(math.log(2.5) - 2.3025851 * jax.random.uniform(streams_of[2], (TOKENS,), jnp.float32) ** levels(streams_of[2], (TOKENS,), ((0, 32),), -0.2, 0.2)), 0.25, 2.5),
        "gate_weight": normal_values(streams_of[3], (EXPERTS, D, FF), D ** -0.5, 0.0625, ((0, 8), (2, 4))),
        "up_weight": normal_values(streams_of[4], (EXPERTS, D, FF), D ** -0.5, 0.0625, ((0, 8), (2, 4))),
        "down_weight": normal_values(streams_of[5], (EXPERTS, FF, D), FF ** -0.5, 0.125, ((0, 8), (1, 4))),
    }


def reference(tokens, target, gate_scale, gate_weight, up_weight, down_weight):
    slot_count = N_GROUP * N_INNER * CAP
    slice_width = FF // N_INNER

    def per_expert(inputs):
        expert_id, gate_mat, up_mat, down_mat = inputs
        is_hit = target == expert_id
        hit_count = jnp.sum(is_hit.astype(jnp.int32))
        row_index = jnp.nonzero(is_hit, size=slot_count, fill_value=0)[0].astype(jnp.int32)
        is_valid = jnp.arange(slot_count, dtype=jnp.int32) < hit_count
        picked = jnp.where(is_valid[:, None], tokens[row_index], jnp.zeros((), tokens.dtype))
        gate_pre = jnp.dot(picked, gate_mat, preferred_element_type=jnp.float32)
        up_pre = jnp.dot(picked, up_mat, preferred_element_type=jnp.float32)
        hidden = (jax.nn.silu(gate_pre) * up_pre).astype(jnp.bfloat16)
        hidden = hidden.reshape(slot_count, N_INNER, slice_width).astype(jnp.float32)
        down_parts = down_mat.reshape(N_INNER, slice_width, D).astype(jnp.float32)
        partials = jnp.einsum("mjk,jkd->mjd", hidden, down_parts).astype(jnp.bfloat16)
        partials = lax.optimization_barrier(partials)
        expert_out = jnp.sum(partials.astype(jnp.float32), axis=1).astype(jnp.bfloat16)
        expert_out = jnp.where(is_valid[:, None], expert_out, jnp.zeros((), expert_out.dtype))
        return row_index, expert_out

    row_index, outputs = lax.map(per_expert, (jnp.arange(N_GROUP, dtype=jnp.int32), gate_weight, up_weight, down_weight))
    scattered = jnp.zeros((TOKENS, D), jnp.float32).at[row_index.reshape(-1)].add(outputs.reshape(-1, D).astype(jnp.float32))
    return (gate_scale[:, None] * scattered).astype(jnp.bfloat16)
```

```python
import functools

import jax
import jax.numpy as jnp
from jax import lax
from jax.experimental import pallas as pl
from jax.experimental.pallas import tpu as pltpu
from jax.sharding import PartitionSpec as P

FOLD = 4
CHUNKS = 4
VMEM_LIMIT = 48 * 1024 * 1024


def slots_of(target_row, me, groups, main):
    tok = target_row.shape[1]
    group_id = lax.broadcasted_iota(jnp.int32, (groups, tok), 0)
    hit = (group_id == target_row).astype(jnp.float32)
    earlier = lax.broadcasted_iota(jnp.int32, (tok, tok), 0) < lax.broadcasted_iota(
        jnp.int32, (tok, tok), 1
    )
    before = jnp.dot(
        hit.astype(jnp.bfloat16),
        earlier.astype(jnp.float32).astype(jnp.bfloat16),
        preferred_element_type=jnp.float32,
    )
    rank = jnp.sum(hit * before, axis=0, keepdims=True).astype(jnp.int32)
    valid = target_row < groups
    base = (target_row ^ me) * main
    main_slot = jnp.where(valid & (rank < main), base + rank, -1)
    tail_slot = jnp.where(valid & (rank >= main), base + rank - main, -(10**6))
    return main_slot, tail_slot


def onehot_rows(slot, rows):
    index = lax.broadcasted_iota(jnp.int32, (rows, slot.shape[1]), 0)
    return (index == slot).astype(jnp.float32).astype(jnp.bfloat16)


def dispatch_kernel(groups, main, me_ref, target_ref, tokens_ref, *out_refs):
    unit = main // FOLD
    rows = groups * main
    width = tokens_ref.shape[1]
    piece = width // FOLD
    main_slot, tail_slot = slots_of(target_ref[...], me_ref[0], groups, main)
    pick_main = onehot_rows(main_slot, rows)
    tail = jnp.zeros((rows, piece), jnp.float32)
    for q in range(FOLD):
        columns = slice(q * piece, (q + 1) * piece)
        block = tokens_ref[:, columns]
        picked = jnp.dot(pick_main, block, preferred_element_type=jnp.float32)
        for k in range(groups):
            out_refs[k][:, columns] = picked[k * main : (k + 1) * main].astype(jnp.bfloat16)
        tail += jnp.dot(
            onehot_rows(tail_slot + q * unit, rows), block, preferred_element_type=jnp.float32
        )
    for k in range(groups):
        out_refs[k][:, width:] = tail[k * main : (k + 1) * main].astype(jnp.bfloat16)


def combine_kernel(groups, main, me_ref, target_ref, scale_ref, *refs):
    back_refs, out_ref = refs[:-1], refs[-1]
    unit = main // FOLD
    rows = groups * main
    tok, width = out_ref.shape
    piece = width // FOLD
    main_slot, tail_slot = slots_of(target_ref[...], me_ref[0], groups, main)
    pick_main = onehot_rows(main_slot, rows)
    square = lax.broadcasted_iota(jnp.int32, (tok, tok), 0) == lax.broadcasted_iota(
        jnp.int32, (tok, tok), 1
    )
    scale = jnp.sum(jnp.where(square, scale_ref[...], 0.0), axis=1, keepdims=True)

    def joined(columns):
        parts = [r[:, columns] for r in back_refs]
        if main % 16 == 0:
            return jnp.concatenate(parts, axis=0)
        return jnp.concatenate([p.astype(jnp.float32) for p in parts], axis=0).astype(jnp.bfloat16)

    tail = joined(slice(width, width + piece))
    over_slots = (((0,), (0,)), ((), ()))
    for q in range(FOLD):
        columns = slice(q * piece, (q + 1) * piece)
        value = lax.dot_general(
            pick_main, joined(columns), over_slots, preferred_element_type=jnp.float32
        )
        value += lax.dot_general(
            onehot_rows(tail_slot + q * unit, rows),
            tail,
            over_slots,
            preferred_element_type=jnp.float32,
        )
        out_ref[:, columns] = (scale * value).astype(jnp.bfloat16)


def expert_kernel(main, parts, gate_ref, up_ref, down_ref, *refs):
    in_refs = refs[:parts]
    keep_ref, send_ref, rows_ref, gate_acc, up_acc, hidden_ref, tail_acc = refs[parts:]
    unit = main // FOLD
    step = pl.program_id(0)
    part_rows = in_refs[0].shape[0]
    rows = parts * part_rows
    half = rows // 2
    tail_rows = rows // FOLD
    piece = gate_ref.shape[0]
    width = piece * FOLD

    def fold_matrix(q):
        tail_id = lax.broadcasted_iota(jnp.int32, (tail_rows, rows), 0)
        folded = lax.broadcasted_iota(jnp.int32, (tail_rows, rows), 1)
        wanted = (tail_id // unit) * main + q * unit + tail_id % unit
        return (wanted == folded).astype(jnp.float32).astype(jnp.bfloat16)

    @pl.when(step == 0)
    def _():
        for a in range(parts):
            for q in range(FOLD):
                rows_ref[q, a * part_rows : (a + 1) * part_rows, :] = in_refs[a][
                    :, q * piece : (q + 1) * piece
                ]
        folded = jnp.concatenate([r[:, width:] for r in in_refs], axis=0)
        for q in range(FOLD):
            rows_ref[q, rows:, :] = jnp.dot(
                fold_matrix(q), folded, preferred_element_type=jnp.float32
            ).astype(jnp.bfloat16)
        gate_acc[...] = jnp.zeros_like(gate_acc)
        up_acc[...] = jnp.zeros_like(up_acc)
        tail_acc[...] = jnp.zeros_like(tail_acc)

    @pl.when(step < FOLD)
    def _():
        block = rows_ref[step]
        gate_acc[...] += jnp.dot(block, gate_ref[...], preferred_element_type=jnp.float32)
        up_acc[...] += jnp.dot(block, up_ref[...], preferred_element_type=jnp.float32)

    @pl.when(step == FOLD - 1)
    def _():
        gate_pre = gate_acc[...]
        hidden_ref[...] = (gate_pre / (1.0 + jnp.exp(-gate_pre)) * up_acc[...]).astype(jnp.bfloat16)

    @pl.when((step >= FOLD) & (step < 2 * FOLD))
    def _():
        partial = jnp.dot(
            hidden_ref[...], down_ref[...], preferred_element_type=jnp.float32
        ).astype(jnp.bfloat16)
        keep_ref[...] = partial[:half]
        send_ref[...] = partial[half:rows]
        tail_acc[...] += lax.dot_general(
            fold_matrix(step - FOLD),
            partial[rows:],
            (((0,), (0,)), ((), ())),
            preferred_element_type=jnp.float32,
        )

    @pl.when(step == 2 * FOLD)
    def _():
        tail = tail_acc[...].astype(jnp.bfloat16)
        keep_ref[...] = tail[:half]
        send_ref[...] = tail[half:]


def run_experts(blocks, gate_mat, up_mat, down_mat, main):
    parts = len(blocks)
    part_rows, folded_width = blocks[0].shape
    width, slice_width = gate_mat.shape
    piece = width // FOLD
    rows = parts * part_rows
    half = rows // 2
    every = rows + rows // FOLD
    whole = pl.BlockSpec((part_rows, folded_width), lambda i: (0, 0))
    into = pl.BlockSpec((piece, slice_width), lambda i: (jnp.minimum(i, FOLD - 1), 0))
    out_of = pl.BlockSpec((slice_width, piece), lambda i: (0, jnp.clip(i - FOLD, 0, FOLD - 1)))
    result = pl.BlockSpec((half, piece), lambda i: (0, jnp.maximum(i - FOLD, 0)))
    return pl.pallas_call(
        functools.partial(expert_kernel, main, parts),
        grid=(2 * FOLD + 1,),
        in_specs=[into, into, out_of] + [whole] * parts,
        out_specs=[result, result],
        out_shape=[jax.ShapeDtypeStruct((half, folded_width), jnp.bfloat16)] * 2,
        scratch_shapes=[
            pltpu.VMEM((FOLD, every, piece), jnp.bfloat16),
            pltpu.VMEM((every, slice_width), jnp.float32),
            pltpu.VMEM((every, slice_width), jnp.float32),
            pltpu.VMEM((every, slice_width), jnp.bfloat16),
            pltpu.VMEM((rows, piece), jnp.float32),
        ],
        compiler_params=pltpu.CompilerParams(vmem_limit_bytes=VMEM_LIMIT),
        cost_estimate=pl.CostEstimate(
            flops=6 * every * width * slice_width,
            bytes_accessed=6 * width * slice_width + 4 * rows * folded_width,
            transcendentals=every * slice_width,
        ),
        name="experts",
    )(gate_mat, up_mat, down_mat, *blocks)


def f32(x):
    return x.astype(jnp.float32)


def body(tokens, target, gate_scale, gate_weight, up_weight, down_weight):
    groups = lax.axis_size("group")
    inner = lax.axis_size("inner")
    chips = inner // 2
    tok_count, width = tokens.shape
    capacity = tok_count * 5 // (4 * groups)
    main = capacity * FOLD // (FOLD + 1)
    folded_width = width + width // FOLD
    per_chunk = groups // CHUNKS

    def to_group(x, offset):
        return lax.ppermute(x, "group", [(i, i ^ offset) for i in range(groups)])

    def to_chip(x, offset):
        return lax.ppermute(x, "inner", [(i, i ^ (2 * offset)) for i in range(inner)])

    def to_core(x):
        return lax.ppermute(x, "inner", [(i, i ^ 1) for i in range(inner)])

    me = lax.axis_index("group").astype(jnp.int32).reshape(1)
    target_row = target.reshape(1, tok_count)
    scalar = pl.BlockSpec(memory_space=pltpu.SMEM)
    vmem = pl.BlockSpec(memory_space=pltpu.VMEM)
    outbound = pl.pallas_call(
        functools.partial(dispatch_kernel, groups, main),
        in_specs=[scalar, vmem, vmem],
        out_specs=[vmem] * groups,
        out_shape=[jax.ShapeDtypeStruct((main, folded_width), jnp.bfloat16)] * groups,
        compiler_params=pltpu.CompilerParams(vmem_limit_bytes=VMEM_LIMIT),
        cost_estimate=pl.CostEstimate(
            flops=4 * tok_count * tok_count * width,
            bytes_accessed=5 * tok_count * width,
            transcendentals=0,
        ),
        name="dispatch",
    )(me, target_row, tokens)

    gate_mat, up_mat, down_mat = gate_weight[0], up_weight[0], down_weight[0]
    back = [None] * groups
    arrived = {}
    for k in sorted(range(groups), key=lambda k: -k):
        arrived[k] = to_group(outbound[k], k) if k else outbound[0]
    for chunk in (0, 1, 3, 2):
        offsets = range(chunk * per_chunk, (chunk + 1) * per_chunk)
        own = jnp.concatenate([arrived[k] for k in offsets], axis=0)
        held = [own] + [to_chip(own, c) for c in range(1, chips)]
        held += [to_core(x) for x in held]
        keep, send = run_experts(held, gate_mat, up_mat, down_mat, main)
        got = to_core(send)
        count = own.shape[0]
        mine = f32(keep[:count]) + f32(got[:count])
        for c in range(1, chips):
            rows = slice(c * count, (c + 1) * count)
            theirs = (f32(keep[rows]) + f32(got[rows])).astype(jnp.bfloat16)
            mine = mine + f32(to_chip(theirs, c))
        finished = mine.astype(jnp.bfloat16)
        for n, k in enumerate(offsets):
            rows = finished[n * main : (n + 1) * main]
            back[k] = to_group(rows, k) if k else rows

    return pl.pallas_call(
        functools.partial(combine_kernel, groups, main),
        in_specs=[scalar] + [vmem] * (2 + groups),
        out_specs=vmem,
        out_shape=jax.ShapeDtypeStruct((tok_count, width), jnp.bfloat16),
        compiler_params=pltpu.CompilerParams(vmem_limit_bytes=VMEM_LIMIT),
        cost_estimate=pl.CostEstimate(
            flops=4 * tok_count * tok_count * width,
            bytes_accessed=5 * tok_count * width,
            transcendentals=0,
        ),
        name="combine",
    )(me, target_row, gate_scale.reshape(1, tok_count), *back)


def solution(mesh):
    in_specs = (
        P(("group", "inner"), None),
        P(("group", "inner")),
        P(("group", "inner")),
        P("group", None, "inner"),
        P("group", None, "inner"),
        P("group", "inner", None),
    )
    out_specs = P(("group", "inner"), None)
    return jax.shard_map(body, mesh=mesh, in_specs=in_specs, out_specs=out_specs, check_vma=False)
```

```python
import functools

import jax
import jax.numpy as jnp
from jax import lax
from jax.experimental import pallas as pl
from jax.experimental.pallas import tpu as pltpu
from jax.sharding import PartitionSpec as P

FOLD = 4
CHUNKS = 4
VMEM_LIMIT = 16 * 1024 * 1024
EXPERT_VMEM = 16 * 1024 * 1024


def slots_of(target_row, me, groups, main):
    tok = target_row.shape[1]
    group_id = lax.broadcasted_iota(jnp.int32, (groups, tok), 0)
    hit = (group_id == target_row).astype(jnp.float32)
    earlier = lax.broadcasted_iota(jnp.int32, (tok, tok), 0) < lax.broadcasted_iota(
        jnp.int32, (tok, tok), 1
    )
    before = jnp.dot(
        hit.astype(jnp.bfloat16),
        earlier.astype(jnp.float32).astype(jnp.bfloat16),
        preferred_element_type=jnp.float32,
    )
    rank = jnp.sum(hit * before, axis=0, keepdims=True).astype(jnp.int32)
    valid = target_row < groups
    base = (target_row ^ me) * main
    main_slot = jnp.where(valid & (rank < main), base + rank, -1)
    tail_slot = jnp.where(valid & (rank >= main), base + rank - main, -(10**6))
    return main_slot, tail_slot


def onehot_rows(slot, rows):
    index = lax.broadcasted_iota(jnp.int32, (rows, slot.shape[1]), 0)
    return (index == slot).astype(jnp.float32).astype(jnp.bfloat16)


def dispatch_kernel(groups, main, me_ref, target_ref, tokens_ref, *out_refs):
    unit = main // FOLD
    rows = groups * main
    width = tokens_ref.shape[1]
    piece = width // FOLD
    main_slot, tail_slot = slots_of(target_ref[...], me_ref[0], groups, main)
    pick_main = onehot_rows(main_slot, rows)
    tail = jnp.zeros((rows, piece), jnp.float32)
    for q in range(FOLD):
        columns = slice(q * piece, (q + 1) * piece)
        block = tokens_ref[:, columns]
        picked = jnp.dot(pick_main, block, preferred_element_type=jnp.float32)
        for k in range(groups):
            out_refs[k][:, columns] = picked[k * main : (k + 1) * main].astype(jnp.bfloat16)
        tail += jnp.dot(
            onehot_rows(tail_slot + q * unit, rows), block, preferred_element_type=jnp.float32
        )
    for k in range(groups):
        out_refs[k][:, width:] = tail[k * main : (k + 1) * main].astype(jnp.bfloat16)


def combine_kernel(groups, main, me_ref, target_ref, scale_ref, *refs):
    back_refs, out_ref = refs[:-2], refs[-1]
    unit = main // FOLD
    rows = groups * main
    tok, width = out_ref.shape
    piece = width // FOLD
    main_slot, tail_slot = slots_of(target_ref[...], me_ref[0], groups, main)
    pick_main = onehot_rows(main_slot, rows)
    square = lax.broadcasted_iota(jnp.int32, (tok, tok), 0) == lax.broadcasted_iota(
        jnp.int32, (tok, tok), 1
    )
    scale = jnp.sum(jnp.where(square, scale_ref[...], 0.0), axis=1, keepdims=True)

    def joined(columns):
        parts = [r[:, columns] for r in back_refs]
        if main % 16 == 0:
            return jnp.concatenate(parts, axis=0)
        return jnp.concatenate([p.astype(jnp.float32) for p in parts], axis=0).astype(jnp.bfloat16)

    tail = joined(slice(width, width + piece))
    over_slots = (((0,), (0,)), ((), ()))
    for q in range(FOLD):
        columns = slice(q * piece, (q + 1) * piece)
        value = lax.dot_general(
            pick_main, joined(columns), over_slots, preferred_element_type=jnp.float32
        )
        value += lax.dot_general(
            onehot_rows(tail_slot + q * unit, rows),
            tail,
            over_slots,
            preferred_element_type=jnp.float32,
        )
        out_ref[:, columns] = (scale * value).astype(jnp.bfloat16)


def expert_kernel(main, parts, gate_ref, up_ref, down_ref, *refs):
    in_refs = refs[:parts]
    keep_ref, send_ref, rows_ref = refs[parts:]
    unit = main // FOLD
    part_rows = in_refs[0].shape[0]
    rows = parts * part_rows
    half = rows // 2
    tail_rows = rows // FOLD
    width = gate_ref.shape[0]
    piece = width // FOLD

    def fold_matrix(q):
        tail_id = lax.broadcasted_iota(jnp.int32, (tail_rows, rows), 0)
        folded = lax.broadcasted_iota(jnp.int32, (tail_rows, rows), 1)
        wanted = (tail_id // unit) * main + q * unit + tail_id % unit
        return (wanted == folded).astype(jnp.float32).astype(jnp.bfloat16)

    folded = jnp.concatenate([r[:, width:] for r in in_refs], axis=0)
    gate_pre = up_pre = None
    for q in range(FOLD):
        columns = slice(q * piece, (q + 1) * piece)
        for a in range(parts):
            rows_ref[a * part_rows : (a + 1) * part_rows, :] = in_refs[a][:, columns]
        rows_ref[rows:, :] = jnp.dot(
            fold_matrix(q), folded, preferred_element_type=jnp.float32
        ).astype(jnp.bfloat16)
        block = rows_ref[...]
        gate_part = jnp.dot(block, gate_ref[columns, :], preferred_element_type=jnp.float32)
        up_part = jnp.dot(block, up_ref[columns, :], preferred_element_type=jnp.float32)
        gate_pre = gate_part if q == 0 else gate_pre + gate_part
        up_pre = up_part if q == 0 else up_pre + up_part
    hidden = (gate_pre / (1.0 + jnp.exp(-gate_pre)) * up_pre).astype(jnp.bfloat16)
    tail = jnp.zeros((rows, piece), jnp.float32)
    for q in range(FOLD):
        columns = slice(q * piece, (q + 1) * piece)
        partial = jnp.dot(
            hidden, down_ref[:, columns], preferred_element_type=jnp.float32
        ).astype(jnp.bfloat16)
        keep_ref[:, columns] = partial[:half]
        send_ref[:, columns] = partial[half:rows]
        tail += lax.dot_general(
            fold_matrix(q),
            partial[rows:],
            (((0,), (0,)), ((), ())),
            preferred_element_type=jnp.float32,
        )
    tail = tail.astype(jnp.bfloat16)
    keep_ref[:, width:] = tail[:half]
    send_ref[:, width:] = tail[half:]


def run_experts(blocks, gate_mat, up_mat, down_mat, main):
    parts = len(blocks)
    part_rows, folded_width = blocks[0].shape
    width, slice_width = gate_mat.shape
    piece = width // FOLD
    rows = parts * part_rows
    half = rows // 2
    every = rows + rows // FOLD
    vmem = pl.BlockSpec(memory_space=pltpu.VMEM)
    return pl.pallas_call(
        functools.partial(expert_kernel, main, parts),
        in_specs=[vmem] * (3 + parts),
        out_specs=[vmem, vmem],
        out_shape=[jax.ShapeDtypeStruct((half, folded_width), jnp.bfloat16)] * 2,
        scratch_shapes=[pltpu.VMEM((every, piece), jnp.bfloat16)],
        compiler_params=pltpu.CompilerParams(vmem_limit_bytes=EXPERT_VMEM),
        cost_estimate=pl.CostEstimate(
            flops=6 * every * width * slice_width,
            bytes_accessed=4 * rows * folded_width,
            transcendentals=every * slice_width,
        ),
        name="experts",
    )(gate_mat, up_mat, down_mat, *blocks)


def loaded(near, *weights):
    def kernel(near_ref, *refs):
        refs[-1][...] = jnp.zeros_like(refs[-1])

    mark = pl.pallas_call(
        kernel,
        in_specs=[pl.BlockSpec(memory_space=pl.ANY)]
        + [pl.BlockSpec(memory_space=pltpu.VMEM)] * len(weights),
        out_specs=pl.BlockSpec(memory_space=pltpu.VMEM),
        out_shape=jax.ShapeDtypeStruct((8, 128), jnp.int32),
        compiler_params=pltpu.CompilerParams(vmem_limit_bytes=EXPERT_VMEM),
        cost_estimate=pl.CostEstimate(
            flops=0, bytes_accessed=sum(2 * w.size for w in weights), transcendentals=0
        ),
        name="loaded",
    )(near, *weights)
    return mark


def together(*values):
    return lax.optimization_barrier(values)


def f32(x):
    return x.astype(jnp.float32)


def body(tokens, target, gate_scale, gate_weight, up_weight, down_weight):
    groups = lax.axis_size("group")
    inner = lax.axis_size("inner")
    chips = inner // 2
    tok_count, width = tokens.shape
    capacity = tok_count * 5 // (4 * groups)
    main = capacity * FOLD // (FOLD + 1)
    folded_width = width + width // FOLD
    per_chunk = groups // CHUNKS

    def to_group(x, offset):
        return lax.ppermute(x, "group", [(i, i ^ offset) for i in range(groups)])

    def to_chip(x, offset):
        return lax.ppermute(x, "inner", [(i, i ^ (2 * offset)) for i in range(inner)])

    def to_core(x):
        return lax.ppermute(x, "inner", [(i, i ^ 1) for i in range(inner)])

    me = lax.axis_index("group").astype(jnp.int32).reshape(1)
    target_row = target.reshape(1, tok_count)
    scalar = pl.BlockSpec(memory_space=pltpu.SMEM)
    vmem = pl.BlockSpec(memory_space=pltpu.VMEM)
    outbound = pl.pallas_call(
        functools.partial(dispatch_kernel, groups, main),
        in_specs=[scalar, vmem, vmem],
        out_specs=[vmem] * groups,
        out_shape=[jax.ShapeDtypeStruct((main, folded_width), jnp.bfloat16)] * groups,
        compiler_params=pltpu.CompilerParams(vmem_limit_bytes=VMEM_LIMIT),
        cost_estimate=pl.CostEstimate(
            flops=4 * tok_count * tok_count * width,
            bytes_accessed=8 * gate_weight.size,
            transcendentals=0,
        ),
        name="dispatch",
    )(me, target_row, tokens)

    gate_mat, up_mat, down_mat = gate_weight[0], up_weight[0], down_weight[0]

    def offsets(chunk):
        return range(chunk * per_chunk, (chunk + 1) * per_chunk)

    def over_chips(own):
        return [own] + [to_chip(own, c) for c in range(1, chips)]

    def stack(parts):
        return jnp.concatenate(list(parts), axis=0)

    def stack_each(lists):
        return [stack(same) for same in zip(*lists)]

    def experts(held):
        held = held + [to_core(x) for x in held]
        keep, send = run_experts(held, gate_mat, up_mat, down_mat, main)
        return keep, to_core(send)

    def chip_sums(keep, got):
        count = keep.shape[0] // chips
        mine = f32(keep[:count]) + f32(got[:count])
        theirs = []
        for c in range(1, chips):
            rows = slice(c * count, (c + 1) * count)
            theirs.append((f32(keep[rows]) + f32(got[rows])).astype(jnp.bfloat16))
        return mine, theirs

    def reduce_chips(mine, theirs):
        for c in range(1, chips):
            mine = mine + f32(to_chip(theirs[c - 1], c))
        return mine.astype(jnp.bfloat16)

    back = [None] * groups

    def return_chunk(chunk, finished):
        for n, k in enumerate(offsets(chunk)):
            rows = finished[n * main : (n + 1) * main]
            back[k] = to_group(rows, k) if k else rows

    arrived3 = [to_group(outbound[k], k) for k in offsets(3)]
    first = over_chips(outbound[0])
    near = [to_group(outbound[k], k) for k in offsets(0) if k]
    relayed = to_group(stack([outbound[k] for k in offsets(1)]), per_chunk)
    mark = loaded(near[-1], gate_mat, up_mat, down_mat)
    held0 = stack_each([first] + [over_chips(x) for x in near])
    outbound2 = [outbound[k] for k in offsets(2)]
    held0[0], mark, relayed, *rest = together(held0[0], mark, relayed, *arrived3, *outbound2)
    arrived3, outbound2 = rest[:per_chunk], rest[per_chunk:]
    keep0, got0 = experts(held0)
    arrived2 = [to_group(x, k) for x, k in zip(outbound2, offsets(2))]
    held3 = over_chips(stack(arrived3))
    arrived1 = [
        to_group(relayed[n * main : (n + 1) * main], n) if n else relayed[:main]
        for n in range(per_chunk)
    ]
    arrived1[-1], keep0 = together(arrived1[-1], keep0)
    held1 = stack_each([over_chips(x) for x in arrived1])
    held3[-1], held1[-1], *arrived2 = together(held3[-1], held1[-1], *arrived2)
    held2 = over_chips(stack(arrived2))
    keep3, got3 = experts(held3)
    mine3, theirs3 = chip_sums(keep3, got3)
    keep1, got1 = experts(held1)
    held2[-1], keep1, *theirs3 = together(held2[-1], keep1, *theirs3)
    keep2, got2 = experts(held2)
    finished3 = reduce_chips(mine3, theirs3)
    mine2, theirs2 = chip_sums(keep2, got2)
    mine1, theirs1 = chip_sums(keep1, got1)
    mine0, theirs0 = chip_sums(keep0, got0)
    finished3, *theirs1 = together(finished3, *theirs1)
    return_chunk(3, finished3)
    finished2 = reduce_chips(mine2, theirs2)
    finished1 = reduce_chips(mine1, theirs1)
    finished2, *theirs0 = together(finished2, *theirs0)
    return_chunk(2, finished2)
    return_chunk(1, finished1)
    finished0 = reduce_chips(mine0, theirs0)
    return_chunk(0, finished0)

    return pl.pallas_call(
        functools.partial(combine_kernel, groups, main),
        in_specs=[scalar] + [vmem] * (2 + groups) + [pl.BlockSpec(memory_space=pl.ANY)],
        out_specs=vmem,
        out_shape=jax.ShapeDtypeStruct((tok_count, width), jnp.bfloat16),
        compiler_params=pltpu.CompilerParams(vmem_limit_bytes=VMEM_LIMIT),
        cost_estimate=pl.CostEstimate(
            flops=4 * tok_count * tok_count * width,
            bytes_accessed=5 * tok_count * width,
            transcendentals=0,
        ),
        name="combine",
    )(me, target_row, gate_scale.reshape(1, tok_count), *back, mark)


def solution(mesh):
    in_specs = (
        P(("group", "inner"), None),
        P(("group", "inner")),
        P(("group", "inner")),
        P("group", None, "inner"),
        P("group", None, "inner"),
        P("group", "inner", None),
    )
    out_specs = P(("group", "inner"), None)
    return jax.shard_map(body, mesh=mesh, in_specs=in_specs, out_specs=out_specs, check_vma=False)
```

```python
import functools

import jax
import jax.numpy as jnp
from jax import lax
from jax.experimental import pallas as pl
from jax.experimental.pallas import tpu as pltpu
from jax.sharding import PartitionSpec as P

FOLD = 4
CHUNKS = 4
VMEM_LIMIT = 16 * 1024 * 1024
EXPERT_VMEM = 16 * 1024 * 1024


ORDER = (
    "S.g30 S.y0 S.x00 S.g1 S.g31 L.g D.y0 S.x01 S.y2 L.u D.x00 D.x01 S.c0 S.c0x L.d D.y2 D.c0 D.c0x "
    "D.g30 D.g31 D.g1 S.g2 S.x31 S.y1 S.x30 S.x10 D.x30 E.0 S.b0 S.c3 D.x31 D.y1 S.c3x S.x11 D.b0 D.x10 "
    "D.c3 D.c3x E.3 S.b3 D.x11 S.c1 S.c1x D.g2 S.x2 D.c1x D.b3 D.c1 S.c2 S.r3 E.1 S.b1 D.c2 D.b1 D.x2 "
    "S.c2x D.c2x E.2 S.b2 D.r3 D.b2 S.h30 S.h31 S.r1 S.r2 D.r1 S.r0 D.h31 S.h1 D.r2 S.h20 S.h21 D.r0 "
    "S.h0 D.h30 D.h1 D.h20 D.h21 D.h0"
).split()


def slots_of(target_row, me, groups, main):
    tok = target_row.shape[1]
    group_id = lax.broadcasted_iota(jnp.int32, (groups, tok), 0)
    hit = (group_id == target_row).astype(jnp.float32)
    earlier = lax.broadcasted_iota(jnp.int32, (tok, tok), 0) < lax.broadcasted_iota(
        jnp.int32, (tok, tok), 1
    )
    before = jnp.dot(
        hit.astype(jnp.bfloat16),
        earlier.astype(jnp.float32).astype(jnp.bfloat16),
        preferred_element_type=jnp.float32,
    )
    rank = jnp.sum(hit * before, axis=0, keepdims=True).astype(jnp.int32)
    valid = target_row < groups
    base = (target_row ^ me) * main
    main_slot = jnp.where(valid & (rank < main), base + rank, -1)
    tail_slot = jnp.where(valid & (rank >= main), base + rank - main, -(10**6))
    return main_slot, tail_slot


def onehot_rows(slot, rows):
    index = lax.broadcasted_iota(jnp.int32, (rows, slot.shape[1]), 0)
    return (index == slot).astype(jnp.float32).astype(jnp.bfloat16)


def dispatch_kernel(groups, main, me_ref, target_ref, tokens_ref, *out_refs):
    unit = main // FOLD
    rows = groups * main
    width = tokens_ref.shape[1]
    piece = width // FOLD
    main_slot, tail_slot = slots_of(target_ref[...], me_ref[0], groups, main)
    pick_main = onehot_rows(main_slot, rows)
    tail = jnp.zeros((rows, piece), jnp.float32)
    for q in range(FOLD):
        columns = slice(q * piece, (q + 1) * piece)
        block = tokens_ref[:, columns]
        picked = jnp.dot(pick_main, block, preferred_element_type=jnp.float32)
        for k in range(groups):
            out_refs[k][:, columns] = picked[k * main : (k + 1) * main].astype(jnp.bfloat16)
        tail += jnp.dot(
            onehot_rows(tail_slot + q * unit, rows), block, preferred_element_type=jnp.float32
        )
    for k in range(groups):
        out_refs[k][:, width:] = tail[k * main : (k + 1) * main].astype(jnp.bfloat16)
    out_refs[groups][...] = jnp.zeros_like(out_refs[groups])


def combine_kernel(groups, main, me_ref, target_ref, scale_ref, *refs):
    back_refs, out_ref = refs[:-2], refs[-1]
    unit = main // FOLD
    rows = groups * main
    tok, width = out_ref.shape
    piece = width // FOLD
    main_slot, tail_slot = slots_of(target_ref[...], me_ref[0], groups, main)
    pick_main = onehot_rows(main_slot, rows)
    square = lax.broadcasted_iota(jnp.int32, (tok, tok), 0) == lax.broadcasted_iota(
        jnp.int32, (tok, tok), 1
    )
    scale = jnp.sum(jnp.where(square, scale_ref[...], 0.0), axis=1, keepdims=True)

    def joined(columns):
        parts = [r[:, columns] for r in back_refs]
        if main % 16 == 0:
            return jnp.concatenate(parts, axis=0)
        return jnp.concatenate([p.astype(jnp.float32) for p in parts], axis=0).astype(jnp.bfloat16)

    tail = joined(slice(width, width + piece))
    over_slots = (((0,), (0,)), ((), ()))
    for q in range(FOLD):
        columns = slice(q * piece, (q + 1) * piece)
        value = lax.dot_general(
            pick_main, joined(columns), over_slots, preferred_element_type=jnp.float32
        )
        value += lax.dot_general(
            onehot_rows(tail_slot + q * unit, rows),
            tail,
            over_slots,
            preferred_element_type=jnp.float32,
        )
        out_ref[:, columns] = (scale * value).astype(jnp.bfloat16)


def expert_kernel(main, parts, gate_ref, up_ref, down_ref, *refs):
    in_refs = refs[:parts]
    keep_ref, send_ref, rows_ref = refs[parts:]
    unit = main // FOLD
    part_rows = in_refs[0].shape[0]
    rows = parts * part_rows
    half = rows // 2
    tail_rows = rows // FOLD
    width = gate_ref.shape[0]
    piece = width // FOLD

    def fold_matrix(q):
        tail_id = lax.broadcasted_iota(jnp.int32, (tail_rows, rows), 0)
        folded = lax.broadcasted_iota(jnp.int32, (tail_rows, rows), 1)
        wanted = (tail_id // unit) * main + q * unit + tail_id % unit
        return (wanted == folded).astype(jnp.float32).astype(jnp.bfloat16)

    folded = jnp.concatenate([r[:, width:] for r in in_refs], axis=0)
    gate_pre = up_pre = None
    for q in range(FOLD):
        columns = slice(q * piece, (q + 1) * piece)
        for a in range(parts):
            rows_ref[a * part_rows : (a + 1) * part_rows, :] = in_refs[a][:, columns]
        rows_ref[rows:, :] = jnp.dot(
            fold_matrix(q), folded, preferred_element_type=jnp.float32
        ).astype(jnp.bfloat16)
        block = rows_ref[...]
        gate_part = jnp.dot(block, gate_ref[columns, :], preferred_element_type=jnp.float32)
        up_part = jnp.dot(block, up_ref[columns, :], preferred_element_type=jnp.float32)
        gate_pre = gate_part if q == 0 else gate_pre + gate_part
        up_pre = up_part if q == 0 else up_pre + up_part
    hidden = (gate_pre / (1.0 + jnp.exp(-gate_pre)) * up_pre).astype(jnp.bfloat16)
    tail = jnp.zeros((rows, piece), jnp.float32)
    for q in range(FOLD):
        columns = slice(q * piece, (q + 1) * piece)
        partial = jnp.dot(
            hidden, down_ref[:, columns], preferred_element_type=jnp.float32
        ).astype(jnp.bfloat16)
        keep_ref[:, columns] = partial[:half]
        send_ref[:, columns] = partial[half:rows]
        tail += lax.dot_general(
            fold_matrix(q),
            partial[rows:],
            (((0,), (0,)), ((), ())),
            preferred_element_type=jnp.float32,
        )
    tail = tail.astype(jnp.bfloat16)
    keep_ref[:, width:] = tail[:half]
    send_ref[:, width:] = tail[half:]


def run_experts(blocks, gate_mat, up_mat, down_mat, main):
    parts = len(blocks)
    part_rows, folded_width = blocks[0].shape
    width, slice_width = gate_mat.shape
    piece = width // FOLD
    rows = parts * part_rows
    half = rows // 2
    every = rows + rows // FOLD
    vmem = pl.BlockSpec(memory_space=pltpu.VMEM)
    return pl.pallas_call(
        functools.partial(expert_kernel, main, parts),
        in_specs=[vmem] * (3 + parts),
        out_specs=[vmem, vmem],
        out_shape=[jax.ShapeDtypeStruct((half, folded_width), jnp.bfloat16)] * 2,
        scratch_shapes=[pltpu.VMEM((every, piece), jnp.bfloat16)],
        compiler_params=pltpu.CompilerParams(vmem_limit_bytes=EXPERT_VMEM),
        cost_estimate=pl.CostEstimate(
            flops=6 * every * width * slice_width,
            bytes_accessed=4 * rows * folded_width,
            transcendentals=every * slice_width,
        ),
        name="experts",
    )(gate_mat, up_mat, down_mat, *blocks)


def loaded(mark, weight):
    def kernel(mark_ref, weight_ref, out_ref):
        out_ref[...] = mark_ref[...]

    vmem = pl.BlockSpec(memory_space=pltpu.VMEM)
    return pl.pallas_call(
        kernel,
        in_specs=[vmem, vmem],
        out_specs=vmem,
        out_shape=jax.ShapeDtypeStruct(mark.shape, mark.dtype),
        compiler_params=pltpu.CompilerParams(vmem_limit_bytes=EXPERT_VMEM),
        cost_estimate=pl.CostEstimate(
            flops=0, bytes_accessed=2 * weight.size, transcendentals=0
        ),
        name="loaded",
    )(mark, weight)


def together(*values):
    return lax.optimization_barrier(values)


def f32(x):
    return x.astype(jnp.float32)


def body(tokens, target, gate_scale, gate_weight, up_weight, down_weight):
    groups = lax.axis_size("group")
    inner = lax.axis_size("inner")
    chips = inner // 2
    tok_count, width = tokens.shape
    capacity = tok_count * 5 // (4 * groups)
    main = capacity * FOLD // (FOLD + 1)
    folded_width = width + width // FOLD
    per_chunk = groups // CHUNKS

    def to_group(x, offset):
        return lax.ppermute(x, "group", [(i, i ^ offset) for i in range(groups)])

    def to_chip(x, offset):
        return lax.ppermute(x, "inner", [(i, i ^ (2 * offset)) for i in range(inner)])

    def to_core(x):
        return lax.ppermute(x, "inner", [(i, i ^ 1) for i in range(inner)])

    me = lax.axis_index("group").astype(jnp.int32).reshape(1)
    target_row = target.reshape(1, tok_count)
    scalar = pl.BlockSpec(memory_space=pltpu.SMEM)
    vmem = pl.BlockSpec(memory_space=pltpu.VMEM)
    *outbound, mark = pl.pallas_call(
        functools.partial(dispatch_kernel, groups, main),
        in_specs=[scalar, vmem, vmem],
        out_specs=[vmem] * (groups + 1),
        out_shape=[jax.ShapeDtypeStruct((main, folded_width), jnp.bfloat16)] * groups
        + [jax.ShapeDtypeStruct((8, 128), jnp.int32)],
        compiler_params=pltpu.CompilerParams(vmem_limit_bytes=VMEM_LIMIT),
        cost_estimate=pl.CostEstimate(
            flops=4 * tok_count * tok_count * width,
            bytes_accessed=8 * gate_weight.size,
            transcendentals=0,
        ),
        name="dispatch",
    )(me, target_row, tokens)

    gate_mat, up_mat, down_mat = gate_weight[0], up_weight[0], down_weight[0]

    def stack(parts):
        return jnp.concatenate(list(parts), axis=0)

    def cut(x, rows):
        return [x[at : at + rows] for at in range(0, x.shape[0], rows)]

    def step(*values):
        nonlocal mark
        *values, mark = together(*values, mark)
        return values

    def to_chips(x):
        return [to_chip(step(x)[0], c) for c in range(1, chips)]

    def to_chips_each(parts):
        return [to_chip(step(x)[0], c + 1) for c, x in enumerate(parts)]

    half = per_chunk // 2
    near = range(1, per_chunk)

    def chunk_rows(chunk):
        return outbound[chunk * per_chunk : (chunk + 1) * per_chunk]

    def to_groups(rows, offsets):
        return [to_group(step(x)[0], k) if k else x for x, k in zip(rows, offsets)]

    def halves(chunk):
        first = chunk * per_chunk
        return range(first, first + half), range(first + half, first + per_chunk)

    own = {"00": [outbound[0]]}
    chip = {}
    held = {}
    got, keep, sums = {}, {}, {}

    def expert_rows(chunk, mine, others):
        held[chunk] = [stack(mine)] + [stack(parts) for parts in zip(*others)]

    def start(name):
        kind, n = name[0], name[1:]
        if name == "y0":
            return to_groups(chunk_rows(0)[1:], near)
        if name == "y2":
            return to_groups(chunk_rows(2)[1:], near)
        if name == "y1":
            return to_groups(got["g1"][1:], near)
        if name == "g1":
            return [to_group(step(stack(chunk_rows(1)))[0], per_chunk)]
        if name == "g2":
            rows = stack(chunk_rows(2)[:1] + got["y2"])
            return [to_group(step(rows)[0], 2 * per_chunk)]
        if kind == "g":
            part = halves(3)[int(n[1])]
            return to_groups([outbound[k] for k in part], part)
        if kind == "x":
            return to_chips(stack(own[n]))
        if kind == "c":
            if n[1:] == "x":
                return [to_core(step(x)[0]) for x in held[n[0]][1:]]
            return [to_core(step(held_own(n))[0])]
        if kind == "b":
            return [to_core(keep[n][1])]
        if kind == "r":
            return to_chips_each(sums[n][1:])
        part = {"0": near, "1": range(per_chunk)}.get(n)
        if part is None:
            part = range(half) if n[1] == "0" else range(half, per_chunk)
        return to_groups([sums[n[0]][0][k] for k in part], [int(n[0]) * per_chunk + k for k in part])

    def held_own(n):
        parts = {"0": ("00", "01"), "1": ("10", "11"), "2": ("2",), "3": ("30", "31")}[n]
        return stack([x for p in parts for x in own[p]])

    def finish(name):
        kind, n = name[0], name[1:]
        if name == "y0":
            own["01"] = got[name]
        elif name == "g1":
            got[name] = cut(got[name][0], main)
            own["10"] = got[name][:1]
        elif name == "y1":
            own["11"] = got[name]
        elif name == "g2":
            own["2"] = got[name]
        elif kind == "g":
            own[n] = got[name]
        elif kind == "x":
            chip[n] = got[name]
            parts = {"0": ("00", "01"), "1": ("10", "11"), "2": ("2",), "3": ("30", "31")}[n[0]]
            if all(p in chip for p in parts):
                others = [stack(same) for same in zip(*[chip[p] for p in parts])]
                held[n[0]] = [held_own(n[0])] + others
        elif kind == "b":
            kept, came = keep[n][0], got[name][0]
            count = kept.shape[0] // chips
            total = [f32(a) + f32(b) for a, b in zip(cut(kept, count), cut(came, count))]
            sums[n] = total[:1] + [x.astype(jnp.bfloat16) for x in total[1:]]
        elif kind == "r":
            total = sums[n][0]
            for x in got[name]:
                total = total + f32(x)
            sums[n] = [cut(total.astype(jnp.bfloat16), main)]

    flying = {}
    for name in ORDER:
        kind, what = name[0], name[2:]
        if kind == "L":
            mark = loaded(mark, {"g": gate_mat, "u": up_mat, "d": down_mat}[what])
        elif kind == "E":
            rows = step(*held[what], *got["c" + what], *got["c" + what + "x"])
            kept, send = run_experts(rows, gate_mat, up_mat, down_mat, main)
            keep[what] = (kept, step(send)[0])
        elif kind == "S":
            flying[what] = start(what)
        else:
            got[what] = step(*flying.pop(what))
            finish(what)

    back = [sums["0"][0][0]] + got["h0"] + got["h1"]
    for part in ("20", "21", "30", "31"):
        back += got["h" + part]

    return pl.pallas_call(
        functools.partial(combine_kernel, groups, main),
        in_specs=[scalar] + [vmem] * (2 + groups) + [pl.BlockSpec(memory_space=pl.ANY)],
        out_specs=vmem,
        out_shape=jax.ShapeDtypeStruct((tok_count, width), jnp.bfloat16),
        compiler_params=pltpu.CompilerParams(vmem_limit_bytes=VMEM_LIMIT),
        cost_estimate=pl.CostEstimate(
            flops=4 * tok_count * tok_count * width,
            bytes_accessed=5 * tok_count * width,
            transcendentals=0,
        ),
        name="combine",
    )(me, target_row, gate_scale.reshape(1, tok_count), *back, mark)


def solution(mesh):
    in_specs = (
        P(("group", "inner"), None),
        P(("group", "inner")),
        P(("group", "inner")),
        P("group", None, "inner"),
        P("group", None, "inner"),
        P("group", "inner", None),
    )
    out_specs = P(("group", "inner"), None)
    return jax.shard_map(body, mesh=mesh, in_specs=in_specs, out_specs=out_specs, check_vma=False)
```

```python
import functools

import jax
import jax.numpy as jnp
from jax import lax
from jax.experimental import pallas as pl
from jax.experimental.pallas import tpu as pltpu
from jax.sharding import PartitionSpec as P

FOLD = 4
CHUNKS = 4
VMEM_LIMIT = 16 * 1024 * 1024
EXPERT_VMEM = 16 * 1024 * 1024


ORDER = (
    "S.g30", "S.y0", "S.g1", "S.x00", "S.g31", "L.g", "D.y0", "S.y2", "L.u", "S.x01", "D.x00",
    "D.x01", "S.c0", "S.c0x", "L.d", "D.c0", "D.g30", "D.g31", "S.x31", "D.y2", "D.g1", "S.g2",
    "S.y1", "D.c0x", "S.x30", "D.x30", "S.x10", "E.0", "D.x31", "S.b0", "D.b0", "S.c3x", "D.y1",
    "S.x11", "S.c3", "D.c3", "D.x10", "D.c3x", "E.3", "S.b3", "D.x11", "S.c1", "S.c1x", "D.g2",
    "S.x2", "D.c1x", "S.c2", "D.c1", "D.b3", "S.r3", "E.1", "S.b1", "D.b1", "D.x2", "S.c2x",
    "S.r1", "D.c2", "D.c2x", "E.2", "S.b2", "D.r3", "D.b2", "S.h30", "S.h31", "S.r2", "D.h31",
    "S.r0", "D.r1", "S.h1", "D.r2", "S.h20", "S.h21", "D.r0", "S.h0", "D.h30", "D.h20", "D.h21",
    "D.h1", "D.h0",
)


def slots_of(target_row, me, groups, main):
    tok = target_row.shape[1]
    group_id = lax.broadcasted_iota(jnp.int32, (groups, tok), 0)
    hit = (group_id == target_row).astype(jnp.float32)
    earlier = lax.broadcasted_iota(jnp.int32, (tok, tok), 0) < lax.broadcasted_iota(
        jnp.int32, (tok, tok), 1
    )
    before = jnp.dot(
        hit.astype(jnp.bfloat16),
        earlier.astype(jnp.float32).astype(jnp.bfloat16),
        preferred_element_type=jnp.float32,
    )
    rank = jnp.sum(hit * before, axis=0, keepdims=True).astype(jnp.int32)
    valid = target_row < groups
    base = (target_row ^ me) * main
    main_slot = jnp.where(valid & (rank < main), base + rank, -1)
    tail_slot = jnp.where(valid & (rank >= main), base + rank - main, -(10**6))
    return main_slot, tail_slot


def onehot_rows(slot, rows):
    index = lax.broadcasted_iota(jnp.int32, (rows, slot.shape[1]), 0)
    return (index == slot).astype(jnp.float32).astype(jnp.bfloat16)


def dispatch_kernel(groups, main, me_ref, target_ref, tokens_ref, *out_refs):
    unit = main // FOLD
    rows = groups * main
    width = tokens_ref.shape[1]
    piece = width // FOLD
    main_slot, tail_slot = slots_of(target_ref[...], me_ref[0], groups, main)
    pick_main = onehot_rows(main_slot, rows)
    tail = jnp.zeros((rows, piece), jnp.float32)
    for q in range(FOLD):
        columns = slice(q * piece, (q + 1) * piece)
        block = tokens_ref[:, columns]
        picked = jnp.dot(pick_main, block, preferred_element_type=jnp.float32)
        for k in range(groups):
            out_refs[k][:, columns] = picked[k * main : (k + 1) * main].astype(jnp.bfloat16)
        tail += jnp.dot(
            onehot_rows(tail_slot + q * unit, rows), block, preferred_element_type=jnp.float32
        )
    for k in range(groups):
        out_refs[k][:, width:] = tail[k * main : (k + 1) * main].astype(jnp.bfloat16)
    out_refs[groups][...] = jnp.zeros_like(out_refs[groups])


def combine_kernel(groups, main, me_ref, target_ref, scale_ref, *refs):
    back_refs, out_ref = refs[:-2], refs[-1]
    unit = main // FOLD
    rows = groups * main
    tok, width = out_ref.shape
    piece = width // FOLD
    main_slot, tail_slot = slots_of(target_ref[...], me_ref[0], groups, main)
    pick_main = onehot_rows(main_slot, rows)
    square = lax.broadcasted_iota(jnp.int32, (tok, tok), 0) == lax.broadcasted_iota(
        jnp.int32, (tok, tok), 1
    )
    scale = jnp.sum(jnp.where(square, scale_ref[...], 0.0), axis=1, keepdims=True)

    def joined(columns):
        parts = [r[:, columns] for r in back_refs]
        if main % 16 == 0:
            return jnp.concatenate(parts, axis=0)
        return jnp.concatenate([p.astype(jnp.float32) for p in parts], axis=0).astype(jnp.bfloat16)

    tail = joined(slice(width, width + piece))
    over_slots = (((0,), (0,)), ((), ()))
    for q in range(FOLD):
        columns = slice(q * piece, (q + 1) * piece)
        value = lax.dot_general(
            pick_main, joined(columns), over_slots, preferred_element_type=jnp.float32
        )
        value += lax.dot_general(
            onehot_rows(tail_slot + q * unit, rows),
            tail,
            over_slots,
            preferred_element_type=jnp.float32,
        )
        out_ref[:, columns] = (scale * value).astype(jnp.bfloat16)


def expert_kernel(main, parts, gate_ref, up_ref, down_ref, *refs):
    in_refs = refs[:parts]
    keep_ref, send_ref, rows_ref = refs[parts:]
    unit = main // FOLD
    part_rows = in_refs[0].shape[0]
    rows = parts * part_rows
    half = rows // 2
    tail_rows = rows // FOLD
    width = gate_ref.shape[0]
    piece = width // FOLD

    def fold_matrix(q):
        tail_id = lax.broadcasted_iota(jnp.int32, (tail_rows, rows), 0)
        folded = lax.broadcasted_iota(jnp.int32, (tail_rows, rows), 1)
        wanted = (tail_id // unit) * main + q * unit + tail_id % unit
        return (wanted == folded).astype(jnp.float32).astype(jnp.bfloat16)

    folded = jnp.concatenate([r[:, width:] for r in in_refs], axis=0)
    gate_pre = up_pre = None
    for q in range(FOLD):
        columns = slice(q * piece, (q + 1) * piece)
        for a in range(parts):
            rows_ref[a * part_rows : (a + 1) * part_rows, :] = in_refs[a][:, columns]
        rows_ref[rows:, :] = jnp.dot(
            fold_matrix(q), folded, preferred_element_type=jnp.float32
        ).astype(jnp.bfloat16)
        block = rows_ref[...]
        gate_part = jnp.dot(block, gate_ref[columns, :], preferred_element_type=jnp.float32)
        up_part = jnp.dot(block, up_ref[columns, :], preferred_element_type=jnp.float32)
        gate_pre = gate_part if q == 0 else gate_pre + gate_part
        up_pre = up_part if q == 0 else up_pre + up_part
    hidden = (gate_pre / (1.0 + jnp.exp(-gate_pre)) * up_pre).astype(jnp.bfloat16)
    tail = jnp.zeros((rows, piece), jnp.float32)
    for q in range(FOLD):
        columns = slice(q * piece, (q + 1) * piece)
        partial = jnp.dot(
            hidden, down_ref[:, columns], preferred_element_type=jnp.float32
        ).astype(jnp.bfloat16)
        keep_ref[:, columns] = partial[:half]
        send_ref[:, columns] = partial[half:rows]
        tail += lax.dot_general(
            fold_matrix(q),
            partial[rows:],
            (((0,), (0,)), ((), ())),
            preferred_element_type=jnp.float32,
        )
    tail = tail.astype(jnp.bfloat16)
    keep_ref[:, width:] = tail[:half]
    send_ref[:, width:] = tail[half:]


def run_experts(blocks, gate_mat, up_mat, down_mat, main):
    parts = len(blocks)
    part_rows, folded_width = blocks[0].shape
    width, slice_width = gate_mat.shape
    piece = width // FOLD
    rows = parts * part_rows
    half = rows // 2
    every = rows + rows // FOLD
    vmem = pl.BlockSpec(memory_space=pltpu.VMEM)
    return pl.pallas_call(
        functools.partial(expert_kernel, main, parts),
        in_specs=[vmem] * (3 + parts),
        out_specs=[vmem, vmem],
        out_shape=[jax.ShapeDtypeStruct((half, folded_width), jnp.bfloat16)] * 2,
        scratch_shapes=[pltpu.VMEM((every, piece), jnp.bfloat16)],
        compiler_params=pltpu.CompilerParams(vmem_limit_bytes=EXPERT_VMEM),
        cost_estimate=pl.CostEstimate(
            flops=6 * every * width * slice_width,
            bytes_accessed=4 * rows * folded_width,
            transcendentals=every * slice_width,
        ),
        name="experts",
    )(gate_mat, up_mat, down_mat, *blocks)


def loaded(mark, weight):
    def kernel(mark_ref, weight_ref, out_ref):
        out_ref[...] = mark_ref[...]

    vmem = pl.BlockSpec(memory_space=pltpu.VMEM)
    return pl.pallas_call(
        kernel,
        in_specs=[vmem, vmem],
        out_specs=vmem,
        out_shape=jax.ShapeDtypeStruct(mark.shape, mark.dtype),
        compiler_params=pltpu.CompilerParams(vmem_limit_bytes=EXPERT_VMEM),
        cost_estimate=pl.CostEstimate(
            flops=0, bytes_accessed=2 * weight.size, transcendentals=0
        ),
        name="loaded",
    )(mark, weight)


def together(*values):
    return lax.optimization_barrier(values)


def f32(x):
    return x.astype(jnp.float32)


def body(tokens, target, gate_scale, gate_weight, up_weight, down_weight):
    groups = lax.axis_size("group")
    inner = lax.axis_size("inner")
    chips = inner // 2
    tok_count, width = tokens.shape
    capacity = tok_count * 5 // (4 * groups)
    main = capacity * FOLD // (FOLD + 1)
    folded_width = width + width // FOLD
    per_chunk = groups // CHUNKS

    def to_group(x, offset):
        return lax.ppermute(x, "group", [(i, i ^ offset) for i in range(groups)])

    def to_chip(x, offset):
        return lax.ppermute(x, "inner", [(i, i ^ (2 * offset)) for i in range(inner)])

    def to_core(x):
        return lax.ppermute(x, "inner", [(i, i ^ 1) for i in range(inner)])

    me = lax.axis_index("group").astype(jnp.int32).reshape(1)
    target_row = target.reshape(1, tok_count)
    scalar = pl.BlockSpec(memory_space=pltpu.SMEM)
    vmem = pl.BlockSpec(memory_space=pltpu.VMEM)
    *outbound, mark = pl.pallas_call(
        functools.partial(dispatch_kernel, groups, main),
        in_specs=[scalar, vmem, vmem],
        out_specs=[vmem] * (groups + 1),
        out_shape=[jax.ShapeDtypeStruct((main, folded_width), jnp.bfloat16)] * groups
        + [jax.ShapeDtypeStruct((8, 128), jnp.int32)],
        compiler_params=pltpu.CompilerParams(vmem_limit_bytes=VMEM_LIMIT),
        cost_estimate=pl.CostEstimate(
            flops=4 * tok_count * tok_count * width,
            bytes_accessed=8 * gate_weight.size,
            transcendentals=0,
        ),
        name="dispatch",
    )(me, target_row, tokens)

    gate_mat, up_mat, down_mat = gate_weight[0], up_weight[0], down_weight[0]

    def stack(parts):
        return jnp.concatenate(list(parts), axis=0)

    def cut(x, rows):
        return [x[at : at + rows] for at in range(0, x.shape[0], rows)]

    def step(*values):
        nonlocal mark
        *values, mark = together(*values, mark)
        return values

    def to_chips(x):
        return [to_chip(step(x)[0], c) for c in range(1, chips)]

    def to_chips_each(parts):
        return [to_chip(step(x)[0], c + 1) for c, x in enumerate(parts)]

    half = per_chunk // 2
    near = range(1, per_chunk)

    def chunk_rows(chunk):
        return outbound[chunk * per_chunk : (chunk + 1) * per_chunk]

    def to_groups(rows, offsets):
        return [to_group(step(x)[0], k) if k else x for x, k in zip(rows, offsets)]

    def halves(chunk):
        first = chunk * per_chunk
        return range(first, first + half), range(first + half, first + per_chunk)

    own = {"00": [outbound[0]]}
    chip = {}
    held = {}
    got, keep, sums = {}, {}, {}

    def expert_rows(chunk, mine, others):
        held[chunk] = [stack(mine)] + [stack(parts) for parts in zip(*others)]

    def start(name):
        kind, n = name[0], name[1:]
        if name == "y0":
            return to_groups(chunk_rows(0)[1:], near)
        if name == "y2":
            return to_groups(chunk_rows(2)[1:], near)
        if name == "y1":
            return to_groups(got["g1"][1:], near)
        if name == "g1":
            return [to_group(step(stack(chunk_rows(1)))[0], per_chunk)]
        if name == "g2":
            rows = stack(chunk_rows(2)[:1] + got["y2"])
            return [to_group(step(rows)[0], 2 * per_chunk)]
        if kind == "g":
            part = halves(3)[int(n[1])]
            return to_groups([outbound[k] for k in part], part)
        if kind == "x":
            return to_chips(stack(own[n]))
        if kind == "c":
            if n[1:] == "x":
                return [to_core(step(x)[0]) for x in held[n[0]][1:]]
            return [to_core(step(held_own(n))[0])]
        if kind == "b":
            return [to_core(keep[n][1])]
        if kind == "r":
            return to_chips_each(sums[n][1:])
        part = {"0": near, "1": range(per_chunk)}.get(n)
        if part is None:
            part = range(half) if n[1] == "0" else range(half, per_chunk)
        return to_groups([sums[n[0]][0][k] for k in part], [int(n[0]) * per_chunk + k for k in part])

    def held_own(n):
        parts = {"0": ("00", "01"), "1": ("10", "11"), "2": ("2",), "3": ("30", "31")}[n]
        return stack([x for p in parts for x in own[p]])

    def finish(name):
        kind, n = name[0], name[1:]
        if name == "y0":
            own["01"] = got[name]
        elif name == "g1":
            got[name] = cut(got[name][0], main)
            own["10"] = got[name][:1]
        elif name == "y1":
            own["11"] = got[name]
        elif name == "g2":
            own["2"] = got[name]
        elif kind == "g":
            own[n] = got[name]
        elif kind == "x":
            chip[n] = got[name]
            parts = {"0": ("00", "01"), "1": ("10", "11"), "2": ("2",), "3": ("30", "31")}[n[0]]
            if all(p in chip for p in parts):
                others = [stack(same) for same in zip(*[chip[p] for p in parts])]
                held[n[0]] = [held_own(n[0])] + others
        elif kind == "b":
            kept, came = keep[n][0], got[name][0]
            count = kept.shape[0] // chips
            total = [f32(a) + f32(b) for a, b in zip(cut(kept, count), cut(came, count))]
            sums[n] = total[:1] + [x.astype(jnp.bfloat16) for x in total[1:]]
        elif kind == "r":
            total = sums[n][0]
            for x in got[name]:
                total = total + f32(x)
            sums[n] = [cut(total.astype(jnp.bfloat16), main)]

    flying = {}
    for name in ORDER:
        kind, what = name[0], name[2:]
        if kind == "L":
            mark = loaded(mark, {"g": gate_mat, "u": up_mat, "d": down_mat}[what])
        elif kind == "E":
            rows = step(*held[what], *got["c" + what], *got["c" + what + "x"])
            kept, send = run_experts(rows, gate_mat, up_mat, down_mat, main)
            keep[what] = (kept, step(send)[0])
        elif kind == "S":
            flying[what] = start(what)
        else:
            got[what] = step(*flying.pop(what))
            finish(what)

    back = [sums["0"][0][0]] + got["h0"] + got["h1"]
    for part in ("20", "21", "30", "31"):
        back += got["h" + part]

    return pl.pallas_call(
        functools.partial(combine_kernel, groups, main),
        in_specs=[scalar] + [vmem] * (2 + groups) + [pl.BlockSpec(memory_space=pl.ANY)],
        out_specs=vmem,
        out_shape=jax.ShapeDtypeStruct((tok_count, width), jnp.bfloat16),
        compiler_params=pltpu.CompilerParams(vmem_limit_bytes=VMEM_LIMIT),
        cost_estimate=pl.CostEstimate(
            flops=4 * tok_count * tok_count * width,
            bytes_accessed=5 * tok_count * width,
            transcendentals=0,
        ),
        name="combine",
    )(me, target_row, gate_scale.reshape(1, tok_count), *back, mark)


def solution(mesh):
    in_specs = (
        P(("group", "inner"), None),
        P(("group", "inner")),
        P(("group", "inner")),
        P("group", None, "inner"),
        P("group", None, "inner"),
        P("group", "inner", None),
    )
    out_specs = P(("group", "inner"), None)
    return jax.shard_map(body, mesh=mesh, in_specs=in_specs, out_specs=out_specs, check_vma=False)
```

```python
import functools

import jax
import jax.numpy as jnp
from jax import lax
from jax.experimental import pallas as pl
from jax.experimental.pallas import tpu as pltpu
from jax.sharding import PartitionSpec as P

FOLD = 4
CHUNKS = 4
VMEM_LIMIT = 16 * 1024 * 1024
EXPERT_VMEM = 16 * 1024 * 1024


ORDER = (
    "S.g31", "S.y0", "S.g30", "S.g1", "S.y2", "S.x00", "L.g", "D.x00", "L.u", "D.y0", "S.x01",
    "S.c0", "D.x01", "S.c0x", "L.d", "D.c0", "D.g31", "S.x31", "D.g1", "D.y2", "S.y1", "S.g2",
    "D.c0x", "D.g30", "E.0", "S.x30", "S.b0", "S.x10", "D.y1", "D.x30", "D.b0", "D.x31",
    "S.c3x", "S.c3", "S.x11", "D.c3", "D.x10", "S.c1", "D.c3x", "E.3", "D.x11", "D.g2", "S.x2",
    "S.c1x", "S.b3", "D.b3", "S.c2", "D.c1", "S.r31", "D.c1x", "E.1", "S.r30", "S.b1", "D.b1",
    "D.x2", "S.c2x", "S.r1", "D.c2", "D.c2x", "E.2", "D.r30", "D.r31", "S.b2", "D.b2", "S.h31",
    "S.h30", "S.r20", "S.r21", "D.h31", "S.r0", "D.r1", "S.h1", "D.r20", "S.h20", "D.r21",
    "S.h21", "D.r0", "S.h0", "D.h30", "D.h20", "D.h21", "D.h1", "D.h0",
)


def slots_of(target_row, me, groups, main):
    tok = target_row.shape[1]
    group_id = lax.broadcasted_iota(jnp.int32, (groups, tok), 0)
    hit = (group_id == target_row).astype(jnp.float32)
    earlier = lax.broadcasted_iota(jnp.int32, (tok, tok), 0) < lax.broadcasted_iota(
        jnp.int32, (tok, tok), 1
    )
    before = jnp.dot(
        hit.astype(jnp.bfloat16),
        earlier.astype(jnp.float32).astype(jnp.bfloat16),
        preferred_element_type=jnp.float32,
    )
    rank = jnp.sum(hit * before, axis=0, keepdims=True).astype(jnp.int32)
    valid = target_row < groups
    base = (target_row ^ me) * main
    main_slot = jnp.where(valid & (rank < main), base + rank, -1)
    tail_slot = jnp.where(valid & (rank >= main), base + rank - main, -(10**6))
    return main_slot, tail_slot


def onehot_rows(slot, rows):
    index = lax.broadcasted_iota(jnp.int32, (rows, slot.shape[1]), 0)
    return (index == slot).astype(jnp.float32).astype(jnp.bfloat16)


def dispatch_kernel(groups, main, me_ref, target_ref, tokens_ref, *out_refs):
    unit = main // FOLD
    rows = groups * main
    width = tokens_ref.shape[1]
    piece = width // FOLD
    main_slot, tail_slot = slots_of(target_ref[...], me_ref[0], groups, main)
    pick_main = onehot_rows(main_slot, rows)
    tail = jnp.zeros((rows, piece), jnp.float32)
    for q in range(FOLD):
        columns = slice(q * piece, (q + 1) * piece)
        block = tokens_ref[:, columns]
        picked = jnp.dot(pick_main, block, preferred_element_type=jnp.float32)
        for k in range(groups):
            out_refs[k][:, columns] = picked[k * main : (k + 1) * main].astype(jnp.bfloat16)
        tail += jnp.dot(
            onehot_rows(tail_slot + q * unit, rows), block, preferred_element_type=jnp.float32
        )
    for k in range(groups):
        out_refs[k][:, width:] = tail[k * main : (k + 1) * main].astype(jnp.bfloat16)
    out_refs[groups][...] = jnp.zeros_like(out_refs[groups])


def combine_kernel(groups, main, me_ref, target_ref, scale_ref, *refs):
    back_refs, out_ref = refs[:-2], refs[-1]
    unit = main // FOLD
    rows = groups * main
    tok, width = out_ref.shape
    piece = width // FOLD
    main_slot, tail_slot = slots_of(target_ref[...], me_ref[0], groups, main)
    pick_main = onehot_rows(main_slot, rows)
    square = lax.broadcasted_iota(jnp.int32, (tok, tok), 0) == lax.broadcasted_iota(
        jnp.int32, (tok, tok), 1
    )
    scale = jnp.sum(jnp.where(square, scale_ref[...], 0.0), axis=1, keepdims=True)

    def joined(columns):
        parts = [r[:, columns] for r in back_refs]
        if main % 16 == 0:
            return jnp.concatenate(parts, axis=0)
        return jnp.concatenate([p.astype(jnp.float32) for p in parts], axis=0).astype(jnp.bfloat16)

    tail = joined(slice(width, width + piece))
    over_slots = (((0,), (0,)), ((), ()))
    for q in range(FOLD):
        columns = slice(q * piece, (q + 1) * piece)
        value = lax.dot_general(
            pick_main, joined(columns), over_slots, preferred_element_type=jnp.float32
        )
        value += lax.dot_general(
            onehot_rows(tail_slot + q * unit, rows),
            tail,
            over_slots,
            preferred_element_type=jnp.float32,
        )
        out_ref[:, columns] = (scale * value).astype(jnp.bfloat16)


def expert_kernel(main, parts, gate_ref, up_ref, down_ref, *refs):
    in_refs = refs[:parts]
    keep_ref, send_ref, rows_ref = refs[parts:]
    unit = main // FOLD
    part_rows = in_refs[0].shape[0]
    rows = parts * part_rows
    half = rows // 2
    tail_rows = rows // FOLD
    width = gate_ref.shape[0]
    piece = width // FOLD

    def fold_matrix(q):
        tail_id = lax.broadcasted_iota(jnp.int32, (tail_rows, rows), 0)
        folded = lax.broadcasted_iota(jnp.int32, (tail_rows, rows), 1)
        wanted = (tail_id // unit) * main + q * unit + tail_id % unit
        return (wanted == folded).astype(jnp.float32).astype(jnp.bfloat16)

    folded = jnp.concatenate([r[:, width:] for r in in_refs], axis=0)
    gate_pre = up_pre = None
    for q in range(FOLD):
        columns = slice(q * piece, (q + 1) * piece)
        for a in range(parts):
            rows_ref[a * part_rows : (a + 1) * part_rows, :] = in_refs[a][:, columns]
        rows_ref[rows:, :] = jnp.dot(
            fold_matrix(q), folded, preferred_element_type=jnp.float32
        ).astype(jnp.bfloat16)
        block = rows_ref[...]
        gate_part = jnp.dot(block, gate_ref[columns, :], preferred_element_type=jnp.float32)
        up_part = jnp.dot(block, up_ref[columns, :], preferred_element_type=jnp.float32)
        gate_pre = gate_part if q == 0 else gate_pre + gate_part
        up_pre = up_part if q == 0 else up_pre + up_part
    hidden = (gate_pre / (1.0 + jnp.exp(-gate_pre)) * up_pre).astype(jnp.bfloat16)
    tail = jnp.zeros((rows, piece), jnp.float32)
    for q in range(FOLD):
        columns = slice(q * piece, (q + 1) * piece)
        partial = jnp.dot(
            hidden, down_ref[:, columns], preferred_element_type=jnp.float32
        ).astype(jnp.bfloat16)
        keep_ref[:, columns] = partial[:half]
        send_ref[:, columns] = partial[half:rows]
        tail += lax.dot_general(
            fold_matrix(q),
            partial[rows:],
            (((0,), (0,)), ((), ())),
            preferred_element_type=jnp.float32,
        )
    tail = tail.astype(jnp.bfloat16)
    keep_ref[:, width:] = tail[:half]
    send_ref[:, width:] = tail[half:]


def run_experts(blocks, gate_mat, up_mat, down_mat, main):
    parts = len(blocks)
    part_rows, folded_width = blocks[0].shape
    width, slice_width = gate_mat.shape
    piece = width // FOLD
    rows = parts * part_rows
    half = rows // 2
    every = rows + rows // FOLD
    vmem = pl.BlockSpec(memory_space=pltpu.VMEM)
    return pl.pallas_call(
        functools.partial(expert_kernel, main, parts),
        in_specs=[vmem] * (3 + parts),
        out_specs=[vmem, vmem],
        out_shape=[jax.ShapeDtypeStruct((half, folded_width), jnp.bfloat16)] * 2,
        scratch_shapes=[pltpu.VMEM((every, piece), jnp.bfloat16)],
        compiler_params=pltpu.CompilerParams(vmem_limit_bytes=EXPERT_VMEM),
        cost_estimate=pl.CostEstimate(
            flops=6 * every * width * slice_width,
            bytes_accessed=4 * rows * folded_width,
            transcendentals=every * slice_width,
        ),
        name="experts",
    )(gate_mat, up_mat, down_mat, *blocks)


def loaded(mark, weight):
    def kernel(mark_ref, weight_ref, out_ref):
        out_ref[...] = mark_ref[...]

    vmem = pl.BlockSpec(memory_space=pltpu.VMEM)
    return pl.pallas_call(
        kernel,
        in_specs=[vmem, vmem],
        out_specs=vmem,
        out_shape=jax.ShapeDtypeStruct(mark.shape, mark.dtype),
        compiler_params=pltpu.CompilerParams(vmem_limit_bytes=EXPERT_VMEM),
        cost_estimate=pl.CostEstimate(
            flops=0, bytes_accessed=2 * weight.size, transcendentals=0
        ),
        name="loaded",
    )(mark, weight)


def together(*values):
    return lax.optimization_barrier(values)


def f32(x):
    return x.astype(jnp.float32)


def body(tokens, target, gate_scale, gate_weight, up_weight, down_weight):
    groups = lax.axis_size("group")
    inner = lax.axis_size("inner")
    chips = inner // 2
    tok_count, width = tokens.shape
    capacity = tok_count * 5 // (4 * groups)
    main = capacity * FOLD // (FOLD + 1)
    folded_width = width + width // FOLD
    per_chunk = groups // CHUNKS

    def to_group(x, offset):
        return lax.ppermute(x, "group", [(i, i ^ offset) for i in range(groups)])

    def to_chip(x, offset):
        return lax.ppermute(x, "inner", [(i, i ^ (2 * offset)) for i in range(inner)])

    def to_core(x):
        return lax.ppermute(x, "inner", [(i, i ^ 1) for i in range(inner)])

    me = lax.axis_index("group").astype(jnp.int32).reshape(1)
    target_row = target.reshape(1, tok_count)
    scalar = pl.BlockSpec(memory_space=pltpu.SMEM)
    vmem = pl.BlockSpec(memory_space=pltpu.VMEM)
    *outbound, mark = pl.pallas_call(
        functools.partial(dispatch_kernel, groups, main),
        in_specs=[scalar, vmem, vmem],
        out_specs=[vmem] * (groups + 1),
        out_shape=[jax.ShapeDtypeStruct((main, folded_width), jnp.bfloat16)] * groups
        + [jax.ShapeDtypeStruct((8, 128), jnp.int32)],
        compiler_params=pltpu.CompilerParams(vmem_limit_bytes=VMEM_LIMIT),
        cost_estimate=pl.CostEstimate(
            flops=4 * tok_count * tok_count * width,
            bytes_accessed=8 * gate_weight.size,
            transcendentals=0,
        ),
        name="dispatch",
    )(me, target_row, tokens)

    gate_mat, up_mat, down_mat = gate_weight[0], up_weight[0], down_weight[0]

    def stack(parts):
        return jnp.concatenate(list(parts), axis=0)

    def cut(x, rows):
        return [x[at : at + rows] for at in range(0, x.shape[0], rows)]

    def step(*values):
        nonlocal mark
        *values, mark = together(*values, mark)
        return values

    def to_chips(x):
        return [to_chip(step(x)[0], c) for c in range(1, chips)]

    def to_chips_each(parts):
        return [to_chip(step(x)[0], c + 1) for c, x in enumerate(parts)]

    half = per_chunk // 2
    near = range(1, per_chunk)

    def chunk_rows(chunk):
        return outbound[chunk * per_chunk : (chunk + 1) * per_chunk]

    def to_groups(rows, offsets):
        return [to_group(step(x)[0], k) if k else x for x, k in zip(rows, offsets)]

    def halves(chunk):
        first = chunk * per_chunk
        return range(first, first + half), range(first + half, first + per_chunk)

    own = {"00": [outbound[0]]}
    chip = {}
    held = {}
    got, keep, sums, done = {}, {}, {}, {}

    def expert_rows(chunk, mine, others):
        held[chunk] = [stack(mine)] + [stack(parts) for parts in zip(*others)]

    def part_of(x, n):
        if len(n) == 1:
            return x
        count = x.shape[0] // 2
        return x[:count] if n[1] == "0" else x[count:]

    def returned(n):
        first = int(n[0]) * per_chunk
        if len(n) == 1:
            return range(first, first + per_chunk)
        return range(first, first + half) if n[1] == "0" else range(first + half, first + per_chunk)

    def start(name):
        kind, n = name[0], name[1:]
        if name == "y0":
            return to_groups(chunk_rows(0)[1:], near)
        if name == "y2":
            return to_groups(chunk_rows(2)[1:], near)
        if name == "y1":
            return to_groups(got["g1"][1:], near)
        if name == "g1":
            return [to_group(step(stack(chunk_rows(1)))[0], per_chunk)]
        if name == "g2":
            rows = stack(chunk_rows(2)[:1] + got["y2"])
            return [to_group(step(rows)[0], 2 * per_chunk)]
        if kind == "g":
            part = halves(3)[int(n[1])]
            return to_groups([outbound[k] for k in part], part)
        if kind == "x":
            return to_chips(stack(own[n]))
        if kind == "c":
            if n[1:] == "x":
                return [to_core(step(x)[0]) for x in held[n[0]][1:]]
            return [to_core(step(held_own(n))[0])]
        if kind == "b":
            return [to_core(keep[n][1])]
        if kind == "r":
            return to_chips_each([part_of(x, n) for x in sums[n[0]][1:]])
        return to_groups(cut(done[n], main), returned(n))

    def held_own(n):
        parts = {"0": ("00", "01"), "1": ("10", "11"), "2": ("2",), "3": ("30", "31")}[n]
        return stack([x for p in parts for x in own[p]])

    def finish(name):
        kind, n = name[0], name[1:]
        if name == "y0":
            own["01"] = got[name]
        elif name == "g1":
            got[name] = cut(got[name][0], main)
            own["10"] = got[name][:1]
        elif name == "y1":
            own["11"] = got[name]
        elif name == "g2":
            own["2"] = got[name]
        elif kind == "g":
            own[n] = got[name]
        elif kind == "x":
            chip[n] = got[name]
            parts = {"0": ("00", "01"), "1": ("10", "11"), "2": ("2",), "3": ("30", "31")}[n[0]]
            if all(p in chip for p in parts):
                others = [stack(same) for same in zip(*[chip[p] for p in parts])]
                held[n[0]] = [held_own(n[0])] + others
        elif kind == "b":
            kept, came = keep[n][0], got[name][0]
            count = kept.shape[0] // chips
            total = [f32(a) + f32(b) for a, b in zip(cut(kept, count), cut(came, count))]
            sums[n] = total[:1] + [x.astype(jnp.bfloat16) for x in total[1:]]
        elif kind == "r":
            total = part_of(sums[n[0]][0], n)
            for x in got[name]:
                total = total + f32(x)
            done[n] = total.astype(jnp.bfloat16)

    flying = {}
    for name in ORDER:
        kind, what = name[0], name[2:]
        if kind == "L":
            mark = loaded(mark, {"g": gate_mat, "u": up_mat, "d": down_mat}[what])
        elif kind == "E":
            rows = step(*held[what], *got["c" + what], *got["c" + what + "x"])
            kept, send = run_experts(rows, gate_mat, up_mat, down_mat, main)
            keep[what] = (kept, step(send)[0])
        elif kind == "S":
            flying[what] = start(what)
        else:
            got[what] = step(*flying.pop(what))
            finish(what)

    back = []
    for part in ("0", "1", "20", "21", "30", "31"):
        back += got["h" + part]

    return pl.pallas_call(
        functools.partial(combine_kernel, groups, main),
        in_specs=[scalar] + [vmem] * (2 + groups) + [pl.BlockSpec(memory_space=pl.ANY)],
        out_specs=vmem,
        out_shape=jax.ShapeDtypeStruct((tok_count, width), jnp.bfloat16),
        compiler_params=pltpu.CompilerParams(vmem_limit_bytes=VMEM_LIMIT),
        cost_estimate=pl.CostEstimate(
            flops=4 * tok_count * tok_count * width,
            bytes_accessed=5 * tok_count * width,
            transcendentals=0,
        ),
        name="combine",
    )(me, target_row, gate_scale.reshape(1, tok_count), *back, mark)


def solution(mesh):
    in_specs = (
        P(("group", "inner"), None),
        P(("group", "inner")),
        P(("group", "inner")),
        P("group", None, "inner"),
        P("group", None, "inner"),
        P("group", "inner", None),
    )
    out_specs = P(("group", "inner"), None)
    return jax.shard_map(body, mesh=mesh, in_specs=in_specs, out_specs=out_specs, check_vma=False)
```

```python
import functools

import jax
import jax.numpy as jnp
from jax import lax
from jax.experimental import pallas as pl
from jax.experimental.pallas import tpu as pltpu
from jax.sharding import PartitionSpec as P

FOLD = 4
CHUNKS = 4
VMEM_LIMIT = 16 * 1024 * 1024
EXPERT_VMEM = 16 * 1024 * 1024


ORDER = (
    "S.g31", "S.y0", "S.g30", "S.g1", "S.y2", "S.x00", "L.g", "D.x00", "L.u", "D.y0", "S.x01",
    "S.c0", "D.x01", "S.c0x", "L.d", "D.c0", "D.g31", "S.x31", "D.g1", "D.y2", "S.y1", "S.g2",
    "D.c0x", "D.g30", "E.0", "S.x30", "S.b0", "S.x10", "D.y1", "D.x30", "D.b0", "D.x31",
    "S.c3x", "S.c3", "S.x11", "D.c3", "D.x10", "S.c1", "D.c3x", "E.3", "D.x11", "D.g2", "S.x2",
    "S.c1x", "S.b3", "D.b3", "S.c2", "D.c1", "S.r31", "D.c1x", "E.1", "S.r30", "S.b1", "D.b1",
    "D.x2", "S.c2x", "S.r1", "D.c2", "D.c2x", "E.2", "D.r30", "D.r31", "S.b2", "D.b2", "S.h31",
    "S.h30", "S.r20", "S.r21", "D.h31", "S.r0", "D.r1", "S.h1", "D.r20", "S.h20", "D.r21",
    "S.h21", "D.r0", "S.h0", "D.h30", "D.h20", "D.h21", "D.h1", "D.h0",
)


def slots_of(target_row, me, groups, main):
    tok = target_row.shape[1]
    group_id = lax.broadcasted_iota(jnp.int32, (groups, tok), 0)
    hit = (group_id == target_row).astype(jnp.float32)
    earlier = lax.broadcasted_iota(jnp.int32, (tok, tok), 0) < lax.broadcasted_iota(
        jnp.int32, (tok, tok), 1
    )
    before = jnp.dot(
        hit.astype(jnp.bfloat16),
        earlier.astype(jnp.float32).astype(jnp.bfloat16),
        preferred_element_type=jnp.float32,
    )
    rank = jnp.sum(hit * before, axis=0, keepdims=True).astype(jnp.int32)
    valid = target_row < groups
    base = (target_row ^ me) * main
    main_slot = jnp.where(valid & (rank < main), base + rank, -1)
    tail_slot = jnp.where(valid & (rank >= main), base + rank - main, -(10**6))
    return main_slot, tail_slot


def onehot_rows(slot, rows):
    index = lax.broadcasted_iota(jnp.int32, (rows, slot.shape[1]), 0)
    return (index == slot).astype(jnp.float32).astype(jnp.bfloat16)


def dispatch_kernel(groups, main, me_ref, target_ref, tokens_ref, *out_refs):
    unit = main // FOLD
    rows = groups * main
    width = tokens_ref.shape[1]
    piece = width // FOLD
    main_slot, tail_slot = slots_of(target_ref[...], me_ref[0], groups, main)
    pick_main = onehot_rows(main_slot, rows)
    tail = jnp.zeros((rows, piece), jnp.float32)
    for q in range(FOLD):
        columns = slice(q * piece, (q + 1) * piece)
        block = tokens_ref[:, columns]
        picked = jnp.dot(pick_main, block, preferred_element_type=jnp.float32)
        for k in range(groups):
            out_refs[k][:, columns] = picked[k * main : (k + 1) * main].astype(jnp.bfloat16)
        tail += jnp.dot(
            onehot_rows(tail_slot + q * unit, rows), block, preferred_element_type=jnp.float32
        )
    for k in range(groups):
        out_refs[k][:, width:] = tail[k * main : (k + 1) * main].astype(jnp.bfloat16)
    out_refs[groups][...] = jnp.zeros_like(out_refs[groups])


def combine_kernel(groups, main, me_ref, target_ref, scale_ref, *refs):
    back_refs, (_, out_hbm, out_ref, sems) = refs[:-4], refs[-4:]
    unit = main // FOLD
    rows = groups * main
    tok, piece = out_ref.shape[1:]
    width = piece * FOLD
    main_slot, tail_slot = slots_of(target_ref[...], me_ref[0], groups, main)
    pick_main = onehot_rows(main_slot, rows)
    square = lax.broadcasted_iota(jnp.int32, (tok, tok), 0) == lax.broadcasted_iota(
        jnp.int32, (tok, tok), 1
    )
    scale = jnp.sum(jnp.where(square, scale_ref[...], 0.0), axis=1, keepdims=True)

    def joined(columns):
        parts = [r[:, columns] for r in back_refs]
        if main % 16 == 0:
            return jnp.concatenate(parts, axis=0)
        return jnp.concatenate([p.astype(jnp.float32) for p in parts], axis=0).astype(jnp.bfloat16)

    tail = joined(slice(width, width + piece))
    over_slots = (((0,), (0,)), ((), ()))
    stores = []
    for q in range(FOLD):
        columns = slice(q * piece, (q + 1) * piece)
        value = lax.dot_general(
            pick_main, joined(columns), over_slots, preferred_element_type=jnp.float32
        )
        value += lax.dot_general(
            onehot_rows(tail_slot + q * unit, rows),
            tail,
            over_slots,
            preferred_element_type=jnp.float32,
        )
        out_ref[q] = (scale * value).astype(jnp.bfloat16)
        stores.append(pltpu.make_async_copy(out_ref.at[q], out_hbm.at[:, columns], sems.at[q]))
        stores[q].start()
    for store in stores:
        store.wait()


def expert_kernel(main, parts, gate_ref, up_ref, down_ref, *refs):
    in_refs = refs[:parts]
    keep_ref, send_ref, rows_ref = refs[parts:]
    unit = main // FOLD
    part_rows = in_refs[0].shape[0]
    rows = parts * part_rows
    half = rows // 2
    tail_rows = rows // FOLD
    width = gate_ref.shape[0]
    piece = width // FOLD

    def fold_matrix(q):
        tail_id = lax.broadcasted_iota(jnp.int32, (tail_rows, rows), 0)
        folded = lax.broadcasted_iota(jnp.int32, (tail_rows, rows), 1)
        wanted = (tail_id // unit) * main + q * unit + tail_id % unit
        return (wanted == folded).astype(jnp.float32).astype(jnp.bfloat16)

    folded = jnp.concatenate([r[:, width:] for r in in_refs], axis=0)
    gate_pre = up_pre = None
    for q in range(FOLD):
        columns = slice(q * piece, (q + 1) * piece)
        for a in range(parts):
            rows_ref[a * part_rows : (a + 1) * part_rows, :] = in_refs[a][:, columns]
        rows_ref[rows:, :] = jnp.dot(
            fold_matrix(q), folded, preferred_element_type=jnp.float32
        ).astype(jnp.bfloat16)
        block = rows_ref[...]
        gate_part = jnp.dot(block, gate_ref[columns, :], preferred_element_type=jnp.float32)
        up_part = jnp.dot(block, up_ref[columns, :], preferred_element_type=jnp.float32)
        gate_pre = gate_part if q == 0 else gate_pre + gate_part
        up_pre = up_part if q == 0 else up_pre + up_part
    hidden = (gate_pre / (1.0 + jnp.exp(-gate_pre)) * up_pre).astype(jnp.bfloat16)
    tail = jnp.zeros((rows, piece), jnp.float32)
    for q in range(FOLD):
        columns = slice(q * piece, (q + 1) * piece)
        partial = jnp.dot(
            hidden, down_ref[:, columns], preferred_element_type=jnp.float32
        ).astype(jnp.bfloat16)
        keep_ref[:, columns] = partial[:half]
        send_ref[:, columns] = partial[half:rows]
        tail += lax.dot_general(
            fold_matrix(q),
            partial[rows:],
            (((0,), (0,)), ((), ())),
            preferred_element_type=jnp.float32,
        )
    tail = tail.astype(jnp.bfloat16)
    keep_ref[:, width:] = tail[:half]
    send_ref[:, width:] = tail[half:]


def run_experts(blocks, gate_mat, up_mat, down_mat, main):
    parts = len(blocks)
    part_rows, folded_width = blocks[0].shape
    width, slice_width = gate_mat.shape
    piece = width // FOLD
    rows = parts * part_rows
    half = rows // 2
    every = rows + rows // FOLD
    vmem = pl.BlockSpec(memory_space=pltpu.VMEM)
    return pl.pallas_call(
        functools.partial(expert_kernel, main, parts),
        in_specs=[vmem] * (3 + parts),
        out_specs=[vmem, vmem],
        out_shape=[jax.ShapeDtypeStruct((half, folded_width), jnp.bfloat16)] * 2,
        scratch_shapes=[pltpu.VMEM((every, piece), jnp.bfloat16)],
        compiler_params=pltpu.CompilerParams(vmem_limit_bytes=EXPERT_VMEM),
        cost_estimate=pl.CostEstimate(
            flops=6 * every * width * slice_width,
            bytes_accessed=4 * rows * folded_width,
            transcendentals=every * slice_width,
        ),
        name="experts",
    )(gate_mat, up_mat, down_mat, *blocks)


def loaded(mark, weight):
    def kernel(mark_ref, weight_ref, out_ref):
        out_ref[...] = mark_ref[...]

    vmem = pl.BlockSpec(memory_space=pltpu.VMEM)
    return pl.pallas_call(
        kernel,
        in_specs=[vmem, vmem],
        out_specs=vmem,
        out_shape=jax.ShapeDtypeStruct(mark.shape, mark.dtype),
        compiler_params=pltpu.CompilerParams(vmem_limit_bytes=EXPERT_VMEM),
        cost_estimate=pl.CostEstimate(
            flops=0, bytes_accessed=2 * weight.size, transcendentals=0
        ),
        name="loaded",
    )(mark, weight)


def together(*values):
    return lax.optimization_barrier(values)


def f32(x):
    return x.astype(jnp.float32)


def body(tokens, target, gate_scale, gate_weight, up_weight, down_weight):
    groups = lax.axis_size("group")
    inner = lax.axis_size("inner")
    chips = inner // 2
    tok_count, width = tokens.shape
    capacity = tok_count * 5 // (4 * groups)
    main = capacity * FOLD // (FOLD + 1)
    folded_width = width + width // FOLD
    per_chunk = groups // CHUNKS

    def to_group(x, offset):
        return lax.ppermute(x, "group", [(i, i ^ offset) for i in range(groups)])

    def to_chip(x, offset):
        return lax.ppermute(x, "inner", [(i, i ^ (2 * offset)) for i in range(inner)])

    def to_core(x):
        return lax.ppermute(x, "inner", [(i, i ^ 1) for i in range(inner)])

    me = lax.axis_index("group").astype(jnp.int32).reshape(1)
    target_row = target.reshape(1, tok_count)
    scalar = pl.BlockSpec(memory_space=pltpu.SMEM)
    vmem = pl.BlockSpec(memory_space=pltpu.VMEM)
    *outbound, mark = pl.pallas_call(
        functools.partial(dispatch_kernel, groups, main),
        in_specs=[scalar, vmem, vmem],
        out_specs=[vmem] * (groups + 1),
        out_shape=[jax.ShapeDtypeStruct((main, folded_width), jnp.bfloat16)] * groups
        + [jax.ShapeDtypeStruct((8, 128), jnp.int32)],
        compiler_params=pltpu.CompilerParams(vmem_limit_bytes=VMEM_LIMIT),
        cost_estimate=pl.CostEstimate(
            flops=4 * tok_count * tok_count * width,
            bytes_accessed=8 * gate_weight.size,
            transcendentals=0,
        ),
        name="dispatch",
    )(me, target_row, tokens)

    gate_mat, up_mat, down_mat = gate_weight[0], up_weight[0], down_weight[0]

    def stack(parts):
        return jnp.concatenate(list(parts), axis=0)

    def cut(x, rows):
        return [x[at : at + rows] for at in range(0, x.shape[0], rows)]

    def step(*values):
        nonlocal mark
        *values, mark = together(*values, mark)
        return values

    def to_chips(x):
        return [to_chip(step(x)[0], c) for c in range(1, chips)]

    def to_chips_each(parts):
        return [to_chip(step(x)[0], c + 1) for c, x in enumerate(parts)]

    half = per_chunk // 2
    near = range(1, per_chunk)

    def chunk_rows(chunk):
        return outbound[chunk * per_chunk : (chunk + 1) * per_chunk]

    def to_groups(rows, offsets):
        return [to_group(step(x)[0], k) if k else x for x, k in zip(rows, offsets)]

    def halves(chunk):
        first = chunk * per_chunk
        return range(first, first + half), range(first + half, first + per_chunk)

    own = {"00": [outbound[0]]}
    chip = {}
    held = {}
    got, keep, sums, done = {}, {}, {}, {}

    def expert_rows(chunk, mine, others):
        held[chunk] = [stack(mine)] + [stack(parts) for parts in zip(*others)]

    def part_of(x, n):
        if len(n) == 1:
            return x
        count = x.shape[0] // 2
        return x[:count] if n[1] == "0" else x[count:]

    def returned(n):
        first = int(n[0]) * per_chunk
        if len(n) == 1:
            return range(first, first + per_chunk)
        return range(first, first + half) if n[1] == "0" else range(first + half, first + per_chunk)

    def start(name):
        kind, n = name[0], name[1:]
        if name == "y0":
            return to_groups(chunk_rows(0)[1:], near)
        if name == "y2":
            return to_groups(chunk_rows(2)[1:], near)
        if name == "y1":
            return to_groups(got["g1"][1:], near)
        if name == "g1":
            return [to_group(step(stack(chunk_rows(1)))[0], per_chunk)]
        if name == "g2":
            rows = stack(chunk_rows(2)[:1] + got["y2"])
            return [to_group(step(rows)[0], 2 * per_chunk)]
        if kind == "g":
            part = halves(3)[int(n[1])]
            return to_groups([outbound[k] for k in part], part)
        if kind == "x":
            return to_chips(stack(own[n]))
        if kind == "c":
            if n[1:] == "x":
                return [to_core(step(x)[0]) for x in held[n[0]][1:]]
            return [to_core(step(held_own(n))[0])]
        if kind == "b":
            return [to_core(keep[n][1])]
        if kind == "r":
            return to_chips_each([part_of(x, n) for x in sums[n[0]][1:]])
        return to_groups(cut(done[n], main), returned(n))

    def held_own(n):
        parts = {"0": ("00", "01"), "1": ("10", "11"), "2": ("2",), "3": ("30", "31")}[n]
        return stack([x for p in parts for x in own[p]])

    def finish(name):
        kind, n = name[0], name[1:]
        if name == "y0":
            own["01"] = got[name]
        elif name == "g1":
            got[name] = cut(got[name][0], main)
            own["10"] = got[name][:1]
        elif name == "y1":
            own["11"] = got[name]
        elif name == "g2":
            own["2"] = got[name]
        elif kind == "g":
            own[n] = got[name]
        elif kind == "x":
            chip[n] = got[name]
            parts = {"0": ("00", "01"), "1": ("10", "11"), "2": ("2",), "3": ("30", "31")}[n[0]]
            if all(p in chip for p in parts):
                others = [stack(same) for same in zip(*[chip[p] for p in parts])]
                held[n[0]] = [held_own(n[0])] + others
        elif kind == "b":
            kept, came = keep[n][0], got[name][0]
            count = kept.shape[0] // chips
            total = [f32(a) + f32(b) for a, b in zip(cut(kept, count), cut(came, count))]
            sums[n] = total[:1] + [x.astype(jnp.bfloat16) for x in total[1:]]
        elif kind == "r":
            total = part_of(sums[n[0]][0], n)
            for x in got[name]:
                total = total + f32(x)
            done[n] = total.astype(jnp.bfloat16)

    flying = {}
    for name in ORDER:
        kind, what = name[0], name[2:]
        if kind == "L":
            mark = loaded(mark, {"g": gate_mat, "u": up_mat, "d": down_mat}[what])
        elif kind == "E":
            rows = step(*held[what], *got["c" + what], *got["c" + what + "x"])
            kept, send = run_experts(rows, gate_mat, up_mat, down_mat, main)
            keep[what] = (kept, step(send)[0])
        elif kind == "S":
            flying[what] = start(what)
        else:
            got[what] = step(*flying.pop(what))
            finish(what)

    back = []
    for part in ("0", "1", "20", "21", "30", "31"):
        back += got["h" + part]

    return pl.pallas_call(
        functools.partial(combine_kernel, groups, main),
        in_specs=[scalar] + [vmem] * (2 + groups) + [pl.BlockSpec(memory_space=pl.ANY)],
        out_specs=pl.BlockSpec(memory_space=pltpu.HBM),
        out_shape=jax.ShapeDtypeStruct((tok_count, width), jnp.bfloat16),
        scratch_shapes=[
            pltpu.VMEM((FOLD, tok_count, width // FOLD), jnp.bfloat16),
            pltpu.SemaphoreType.DMA((FOLD,)),
        ],
        compiler_params=pltpu.CompilerParams(vmem_limit_bytes=VMEM_LIMIT),
        cost_estimate=pl.CostEstimate(
            flops=4 * tok_count * tok_count * width,
            bytes_accessed=5 * tok_count * width,
            transcendentals=0,
        ),
        name="combine",
    )(me, target_row, gate_scale.reshape(1, tok_count), *back, mark)


def solution(mesh):
    in_specs = (
        P(("group", "inner"), None),
        P(("group", "inner")),
        P(("group", "inner")),
        P("group", None, "inner"),
        P("group", None, "inner"),
        P("group", "inner", None),
    )
    out_specs = P(("group", "inner"), None)
    return jax.shard_map(body, mesh=mesh, in_specs=in_specs, out_specs=out_specs, check_vma=False)
```
